1024 devices in a mesh: mode: 16 (over x_hi, y, core), slab: 64 (over z, x_lo).
Axes of the slice: x: 4 (x_hi: 2, x_lo: 2; x = x_hi * 2 + x_lo), y: 4, z: 32, core: 2. Of those that a mesh axis runs over, the one named last changes fastest.
Arguments:
- phonons: float32 [4096, 64, 192], P('mode', 'slab'), may hold values from -4 to 4
- speeds: float32 [4096], replicated, may hold values from 0.3 to 1
- upward: int32 [4096], replicated, may hold values from 0 to 1
- courant: float32 [64, 192], P('slab'), may hold values from 0.2 to 0.9
- blocks: bfloat16 [32, 5, 128, 128], replicated, may hold values from -0.25 to 0.25
- block_cols: int32 [32, 5], replicated, may hold values from 0 to 31
- damping: float32 [4096], replicated, may hold values from 0.2 to 1
Outputs:
- evolved: float32 [4096, 64, 192], P('mode', 'slab')
The draws below stay inside these ranges and needn't reach their ends.
Inputs may be any that keep to these rules, and one draw needn't show every extreme that they name: `block_cols`: block columns of a block row may repeat.
All inputs are finite; a program needn't handle non-finite values.
Results may differ from the reference program's by a relative error of at most 0.0011.
Values sent between devices are 32-bit elements; how exact they have to be, the bound alone decides.
No kernel may reach another device: no remote copies, remote signals or barrier semaphores. Data moves between devices by JAX's collectives and lax.ppermute only.
A program may use at most 32 MiB of HBM per device.

```python
import math
import jax
import jax.numpy as jnp
from jax import lax

M = 4096
BLOCK = 128
NNZ = 5
STEPS = 2
CXY = 192
NB = 32
NZ = 64


def touch_ends(array, own_key, least, high):
    place = [jax.random.randint(jax.random.fold_in(own_key, axis), (), 0, length) for axis, length in enumerate(array.shape)]
    longest = array.shape.index(max(array.shape))
    beside = place[:longest] + [(place[longest] + 1) % array.shape[longest]] + place[longest + 1:]
    return array.at[tuple(place)].set(least).at[tuple(beside)].set(high)


def levels(rng, dims, shards, low, largest):
    gain, own = 1.0, jax.random.fold_in(rng, 6)
    for axis_at, blocks in shards:
        heights = jnp.exp(jax.random.uniform(jax.random.fold_in(own, axis_at), (blocks,), jnp.float32, low / len(shards), largest / len(shards)))
        gain = gain * jnp.repeat(heights, dims[axis_at] // blocks).reshape([-1 if axis == axis_at else 1 for axis in range(len(dims))])
    return gain


def scatter_about(rng, dims, deviation, most, shards=(), held_as=jnp.bfloat16):
    values = jax.random.normal(rng, dims, jnp.float32) * deviation
    if len(shards) > 0:
        values = levels(rng, dims, shards, -0.22, 0.18) * values
    return jnp.clip(values, min=-most, max=most).astype(held_as)


def setup_inputs(seed: int = 0) -> dict:
    arg_keys = jax.random.split(jax.random.key(seed), 8)
    phonons = scatter_about(arg_keys[0], (M, NZ, CXY), 1.0, 4.0, ((0, 16), (1, 64)), jnp.float32)
    speeds = jnp.clip(jax.random.uniform(arg_keys[1], (M,), jnp.float32, 0.3, 1.0), 0.3, 1.0)
    upward = touch_ends(jax.random.randint(arg_keys[2], (M,), 0, 2), jax.random.fold_in(arg_keys[2], 1), 0, 1).astype(jnp.int32)
    courant = jnp.clip(0.2 + 0.7 * jax.random.uniform(arg_keys[3], (NZ, CXY), jnp.float32) ** levels(arg_keys[3], (NZ, CXY), ((0, 64),), -0.2, 0.2), 0.2, 0.9)
    blocks = scatter_about(arg_keys[4], (NB, NNZ, BLOCK, BLOCK), (NNZ * BLOCK) ** -0.5, 0.25)
    block_cols = touch_ends(jax.random.randint(arg_keys[5], (NB, NNZ), 0, NB), jax.random.fold_in(arg_keys[5], 1), 0, NB - 1).astype(jnp.int32)
    damping = jnp.clip(jnp.exp(jax.random.uniform(arg_keys[6], (M,), jnp.float32, math.log(0.2), math.log(1.0))), 0.2, 1.0)
    return dict(phonons=phonons, speeds=speeds, upward=upward, courant=courant, blocks=blocks, block_cols=block_cols, damping=damping)


relax_time = 0.25


def advect(field, speeds, upward, courant):
    zeros = jnp.zeros_like(field[:, :1, :])
    lower = jnp.concatenate([zeros, field[:, :-1, :]], axis=1)
    upper = jnp.concatenate([field[:, 1:, :], zeros], axis=1)
    chosen = jnp.where(upward[:, None, None] == 1, lower, upper)
    return field - courant[None] * speeds[:, None, None] * (field - chosen)


def collide_layer(layer, wide_blocks, block_cols, damping):
    rounded = layer.astype(jnp.bfloat16).reshape(NB, BLOCK, layer.shape[1])
    picked = rounded[block_cols].astype(jnp.float32)
    source = jnp.einsum("rkij,rkjc->ric", wide_blocks, picked).reshape(layer.shape)
    return layer + relax_time * (source - damping[:, None] * layer * jnp.abs(layer))


def reference(phonons, speeds, upward, courant, blocks, block_cols, damping):
    wide_blocks = blocks.astype(jnp.float32)
    field = phonons
    for repeat in range(STEPS):
        field = advect(field, speeds, upward, courant)
        layers = jnp.moveaxis(field, 1, 0)
        result = lax.map(lambda layer: collide_layer(layer, wide_blocks, block_cols, damping), layers)
        field = jnp.moveaxis(result, 0, 1)
    return field
```

```python
import jax
import jax.numpy as jnp
from jax import lax
from jax.experimental import pallas as pl
from jax.experimental.pallas import tpu as pltpu
from jax.sharding import Mesh, PartitionSpec as P

MODE = ("xh", "y", "core")
PLANE = ("xh", "y", "core", "xl")
PEERS = 32
COLS = 6
NBLOCK = 32
NNZ = 5
BLOCK = 128
HALO_ROWS = 392
CHUNK = 4
RELAX = 0.25
VMEM_LIMIT = 32 * 1024 * 1024


def pack_kernel(x_ref, c_ref, msg_ref):
    for j in range(PEERS):
        for h in range(2):
            msg_ref[j, 8 * h : 8 * h + 6, :] = x_ref[COLS * j : COLS * j + 6, 128 * h : 128 * h + 128]
        msg_ref[j, 6:7, 0:6] = c_ref[0:1, COLS * j : COLS * j + 6]


def halo_kernel(rec_ref, out_ref):
    for d in range(16):
        for xl in range(2):
            for h in range(2):
                row = 24 * d + 12 * xl + 6 * h
                out_ref[row : row + 8, :] = rec_ref[2 * d + xl, 8 * h : 8 * h + 8, :]
    out_ref[384:385, :] = rec_ref[0, 6:7, :]
    out_ref[385:386, :] = rec_ref[1, 6:7, :]


def on_rows(row):
    lane = lax.broadcasted_iota(jnp.int32, (8, 128), 1)
    cell = lax.broadcasted_iota(jnp.int32, (8, 128), 0)
    picked = jnp.where(lane == cell, jnp.broadcast_to(row, (8, 128)), 0.0)
    return jnp.broadcast_to(jnp.sum(picked, axis=1, keepdims=True), (8, 128))


def steps_kernel(
    cols_ref, rec_ref, low_ref, high_ref, speeds_ref, upward_ref, damping_ref, blocks_hbm,
    out_ref, blocks_ref, adv_ref, rounded_ref, field_ref, adv2_ref, rounded2_ref, sems,
):
    def copy(i):
        part = pl.ds(CHUNK * i, CHUNK)
        return pltpu.make_async_copy(blocks_hbm.at[part], blocks_ref.at[part], sems.at[i])

    for i in range(NBLOCK // CHUNK):
        copy(i).start()

    courant = [
        on_rows(low_ref[385:386, :]),
        on_rows(rec_ref[0, 6:7, :]),
        on_rows(rec_ref[1, 6:7, :]),
        on_rows(high_ref[384:385, :]),
    ]

    for b in range(NBLOCK):
        d, h = divmod(b, 2)
        row = 24 * d + 6 * h
        layers = [
            low_ref[row : row + 8, :],
            low_ref[row + 12 : row + 20, :],
            rec_ref[2 * d, 8 * h : 8 * h + 8, :],
            rec_ref[2 * d + 1, 8 * h : 8 * h + 8, :],
            high_ref[row : row + 8, :],
            high_ref[row + 12 : row + 20, :],
        ]
        speed = speeds_ref[b : b + 1, :]
        up = jnp.broadcast_to(upward_ref[b : b + 1, :], (8, 128)) == 1
        moved = []
        for k in range(4):
            here = layers[k + 1]
            chosen = jnp.where(up, layers[k], layers[k + 2])
            moved.append(here - courant[k] * speed * (here - chosen))
        moved = jnp.concatenate(moved, axis=0)
        adv_ref[b] = moved
        rounded_ref[b] = moved.astype(jnp.bfloat16)

    def source(r, values_ref):
        picked = jnp.concatenate([values_ref[cols_ref[r, k]] for k in range(NNZ)], axis=1)
        stored = jnp.concatenate([blocks_ref[r, k] for k in range(NNZ)], axis=1)
        return lax.dot_general(picked, stored, (((1,), (1,)), ((), ())), preferred_element_type=jnp.float32)

    for r in range(NBLOCK):
        if r % CHUNK == 0:
            copy(r // CHUNK).wait()
        adv = adv_ref[r]
        field_ref[r] = adv + RELAX * (source(r, rounded_ref) - damping_ref[r : r + 1, :] * adv * jnp.abs(adv))

    for b in range(NBLOCK):
        speed = speeds_ref[b : b + 1, :]
        up = jnp.broadcast_to(upward_ref[b : b + 1, :], (8, 128)) == 1
        moved = []
        for k in range(2):
            here = field_ref[b, 8 * k + 8 : 8 * k + 16, :]
            chosen = jnp.where(up, field_ref[b, 8 * k : 8 * k + 8, :], field_ref[b, 8 * k + 16 : 8 * k + 24, :])
            moved.append(here - courant[k + 1] * speed * (here - chosen))
        moved = jnp.concatenate(moved, axis=0)
        adv2_ref[b] = moved
        rounded2_ref[b] = moved.astype(jnp.bfloat16)

    for r in range(NBLOCK):
        d, h = divmod(r, 2)
        adv = adv2_ref[r]
        last = adv + RELAX * (source(r, rounded2_ref) - damping_ref[r : r + 1, :] * adv * jnp.abs(adv))
        out_ref[2 * d, 8 * h : 8 * h + 8, :] = last[0:8]
        out_ref[2 * d + 1, 8 * h : 8 * h + 8, :] = last[8:16]


def unpack_kernel(msg_ref, out_ref):
    for j in range(PEERS):
        for h in range(2):
            out_ref[COLS * j : COLS * j + 6, 128 * h : 128 * h + 128] = msg_ref[j, 8 * h : 8 * h + 6, :]


def vmem():
    return pl.BlockSpec(memory_space=pltpu.VMEM)


PARAMS = dict(compiler_params=pltpu.CompilerParams(vmem_limit_bytes=VMEM_LIMIT))


def on_device(phonons, speeds, upward, courant, blocks, block_cols, damping):
    zs = lax.axis_size("z")
    up = [(i, i + 1) for i in range(zs - 1)]
    down = [(j, i) for i, j in up]
    cells = jnp.transpose(phonons.reshape(256, 192))
    msg_type = jax.ShapeDtypeStruct((PEERS, 16, 128), jnp.float32)

    msg = pl.pallas_call(pack_kernel, out_shape=msg_type, in_specs=[vmem()] * 2, out_specs=vmem(), **PARAMS)(cells, courant)
    rec = lax.all_to_all(msg, PLANE, split_axis=0, concat_axis=0, tiled=True)
    halo = pl.pallas_call(
        halo_kernel, out_shape=jax.ShapeDtypeStruct((HALO_ROWS, 128), jnp.float32), in_specs=[vmem()], out_specs=vmem(), **PARAMS
    )(rec)
    low = lax.ppermute(halo, "z", up)
    high = lax.ppermute(halo, "z", down)
    back = pl.pallas_call(
        steps_kernel,
        out_shape=msg_type,
        in_specs=[pl.BlockSpec(memory_space=pltpu.SMEM)] + [vmem()] * 6 + [pl.BlockSpec(memory_space=pl.ANY)],
        out_specs=vmem(),
        scratch_shapes=[
            pltpu.VMEM((NBLOCK, NNZ, BLOCK, BLOCK), jnp.bfloat16),
            pltpu.VMEM((NBLOCK, 32, 128), jnp.float32),
            pltpu.VMEM((NBLOCK, 32, 128), jnp.bfloat16),
            pltpu.VMEM((NBLOCK, 32, 128), jnp.float32),
            pltpu.VMEM((NBLOCK, 16, 128), jnp.float32),
            pltpu.VMEM((NBLOCK, 16, 128), jnp.bfloat16),
            pltpu.SemaphoreType.DMA((NBLOCK // CHUNK,)),
        ],
        **PARAMS,
    )(
        block_cols, rec, low, high, speeds.reshape(NBLOCK, 128), upward.reshape(NBLOCK, 128),
        damping.reshape(NBLOCK, 128), blocks,
    )
    got = lax.all_to_all(back, PLANE, split_axis=0, concat_axis=0, tiled=True)
    out = pl.pallas_call(
        unpack_kernel, out_shape=jax.ShapeDtypeStruct((192, 256), jnp.float32), in_specs=[vmem()], out_specs=vmem(), **PARAMS
    )(got)
    return jnp.transpose(out).reshape(256, 1, 192)


def solution(mesh):
    fine = Mesh(mesh.devices.reshape(2, 4, 2, 32, 2), ("xh", "y", "core", "z", "xl"))
    return jax.shard_map(
        on_device,
        mesh=fine,
        in_specs=(P(MODE, ("z", "xl"), None), P(), P(), P(("z", "xl"), None), P(), P(), P()),
        out_specs=P(MODE, ("z", "xl"), None),
        check_vma=False,
    )
```

```python
import jax
import jax.numpy as jnp
from jax import lax
from jax.experimental import pallas as pl
from jax.experimental.pallas import tpu as pltpu
from jax.sharding import Mesh, PartitionSpec as P

MODE = ("xh", "y", "core")
PLANE = ("xh", "y", "core", "xl")
PEERS = 32
COLS = 6
NBLOCK = 32
NNZ = 5
BLOCK = 128
HALO_ROWS = 392
CHUNK = 4
PARTS = NBLOCK // CHUNK
RELAX = 0.25
VMEM_LIMIT = 32 * 1024 * 1024


def pack_kernel(x_hbm, c_hbm, msg_ref, x_ref, c_ref, sems):
    copies = [
        pltpu.make_async_copy(x_hbm, x_ref, sems.at[0]),
        pltpu.make_async_copy(c_hbm, c_ref, sems.at[1]),
    ]
    for copy in copies:
        copy.start()
    for copy in copies:
        copy.wait()
    for j in range(PEERS):
        for h in range(2):
            msg_ref[j, 8 * h : 8 * h + 6, :] = x_ref[COLS * j : COLS * j + 6, 128 * h : 128 * h + 128]
        msg_ref[j, 6:7, 0:6] = c_ref[0:1, COLS * j : COLS * j + 6]


def halo_kernel(rec_ref, out_ref):
    for d in range(16):
        for xl in range(2):
            for h in range(2):
                row = 24 * d + 12 * xl + 6 * h
                out_ref[row : row + 8, :] = rec_ref[2 * d + xl, 8 * h : 8 * h + 8, :]
    out_ref[384:385, :] = rec_ref[0, 6:7, :]
    out_ref[385:386, :] = rec_ref[1, 6:7, :]


def on_rows(row):
    lane = lax.broadcasted_iota(jnp.int32, (8, 128), 1)
    cell = lax.broadcasted_iota(jnp.int32, (8, 128), 0)
    picked = jnp.where(lane == cell, jnp.broadcast_to(row, (8, 128)), 0.0)
    return jnp.broadcast_to(jnp.sum(picked, axis=1, keepdims=True), (8, 128))


def prepare_kernel(
    _, blocks_hbm, speeds_hbm, upward_hbm, damping_hbm,
    turned_ref, speeds_ref, upward_ref, damping_ref, blocks_ref, sems,
):
    vectors = [
        pltpu.make_async_copy(speeds_hbm, speeds_ref, sems.at[PARTS]),
        pltpu.make_async_copy(upward_hbm, upward_ref, sems.at[PARTS + 1]),
        pltpu.make_async_copy(damping_hbm, damping_ref, sems.at[PARTS + 2]),
    ]
    copies = []
    for i in range(PARTS):
        part = pl.ds(CHUNK * i, CHUNK)
        copies.append(pltpu.make_async_copy(blocks_hbm.at[part], blocks_ref.at[part], sems.at[i]))
    for copy in copies + vectors:
        copy.start()
    for i in range(PARTS):
        copies[i].wait()
        for r in range(CHUNK * i, CHUNK * i + CHUNK):
            for k in range(NNZ):
                turned_ref[r, BLOCK * k : BLOCK * k + BLOCK, :] = blocks_ref[r, k].T
    for copy in vectors:
        copy.wait()


def steps_kernel(
    cols_ref, rec_ref, low_ref, high_ref, turned_ref, speeds_ref, upward_ref, damping_ref,
    out_ref, adv_ref, rounded_ref, field_ref, adv2_ref, rounded2_ref,
):
    courant = [
        on_rows(low_ref[385:386, :]),
        on_rows(rec_ref[0, 6:7, :]),
        on_rows(rec_ref[1, 6:7, :]),
        on_rows(high_ref[384:385, :]),
    ]

    for b in range(NBLOCK):
        d, h = divmod(b, 2)
        row = 24 * d + 6 * h
        layers = [
            low_ref[row : row + 8, :],
            low_ref[row + 12 : row + 20, :],
            rec_ref[2 * d, 8 * h : 8 * h + 8, :],
            rec_ref[2 * d + 1, 8 * h : 8 * h + 8, :],
            high_ref[row : row + 8, :],
            high_ref[row + 12 : row + 20, :],
        ]
        speed = speeds_ref[b : b + 1, :]
        up = jnp.broadcast_to(upward_ref[b : b + 1, :], (8, 128)) == 1
        moved = []
        for k in range(4):
            here = layers[k + 1]
            chosen = jnp.where(up, layers[k], layers[k + 2])
            moved.append(here - courant[k] * speed * (here - chosen))
        moved = jnp.concatenate(moved, axis=0)
        adv_ref[b] = moved
        rounded_ref[b] = moved.astype(jnp.bfloat16)

    def source(r, values_ref):
        picked = jnp.concatenate([values_ref[cols_ref[k, r]] for k in range(NNZ)], axis=1)
        return jnp.dot(picked, turned_ref[r], preferred_element_type=jnp.float32)

    for r in range(NBLOCK):
        adv = adv_ref[r]
        field_ref[r] = adv + RELAX * (source(r, rounded_ref) - damping_ref[r : r + 1, :] * adv * jnp.abs(adv))

    for b in range(NBLOCK):
        speed = speeds_ref[b : b + 1, :]
        up = jnp.broadcast_to(upward_ref[b : b + 1, :], (8, 128)) == 1
        moved = []
        for k in range(2):
            here = field_ref[b, 8 * k + 8 : 8 * k + 16, :]
            chosen = jnp.where(up, field_ref[b, 8 * k : 8 * k + 8, :], field_ref[b, 8 * k + 16 : 8 * k + 24, :])
            moved.append(here - courant[k + 1] * speed * (here - chosen))
        moved = jnp.concatenate(moved, axis=0)
        adv2_ref[b] = moved
        rounded2_ref[b] = moved.astype(jnp.bfloat16)

    for r in range(NBLOCK):
        d, h = divmod(r, 2)
        adv = adv2_ref[r]
        last = adv + RELAX * (source(r, rounded2_ref) - damping_ref[r : r + 1, :] * adv * jnp.abs(adv))
        out_ref[2 * d, 8 * h : 8 * h + 8, :] = last[0:8]
        out_ref[2 * d + 1, 8 * h : 8 * h + 8, :] = last[8:16]


def unpack_kernel(msg_ref, out_ref):
    for j in range(PEERS):
        for h in range(2):
            out_ref[COLS * j : COLS * j + 6, 128 * h : 128 * h + 128] = msg_ref[j, 8 * h : 8 * h + 6, :]


def vmem():
    return pl.BlockSpec(memory_space=pltpu.VMEM)


def hbm():
    return pl.BlockSpec(memory_space=pltpu.HBM)


def in_hbm(array):
    return pltpu.with_memory_space_constraint(array, pltpu.HBM)


PARAMS = dict(compiler_params=pltpu.CompilerParams(vmem_limit_bytes=VMEM_LIMIT))


def on_device(phonons, speeds, upward, courant, blocks, block_cols, damping):
    zs = lax.axis_size("z")
    up = [(i, i + 1) for i in range(zs - 1)]
    down = [(j, i) for i, j in up]
    cells = jnp.transpose(phonons.reshape(256, 192))
    msg_type = jax.ShapeDtypeStruct((PEERS, 16, 128), jnp.float32)

    msg = pl.pallas_call(
        pack_kernel,
        out_shape=msg_type,
        in_specs=[hbm()] * 2,
        out_specs=vmem(),
        scratch_shapes=[pltpu.VMEM((192, 256), jnp.float32), pltpu.VMEM((1, 192), jnp.float32), pltpu.SemaphoreType.DMA((2,))],
        **PARAMS,
    )(in_hbm(cells), in_hbm(courant))
    rec = lax.all_to_all(msg, PLANE, split_axis=0, concat_axis=0, tiled=True)
    halo = pl.pallas_call(
        halo_kernel, out_shape=jax.ShapeDtypeStruct((HALO_ROWS, 128), jnp.float32), in_specs=[vmem()], out_specs=vmem(), **PARAMS
    )(rec)
    low = lax.ppermute(halo, "z", up)
    high = lax.ppermute(halo, "z", down)
    vector = jax.ShapeDtypeStruct((NBLOCK, 128), jnp.float32)
    prepared = pl.pallas_call(
        prepare_kernel,
        out_shape=[
            jax.ShapeDtypeStruct((NBLOCK, NNZ * BLOCK, BLOCK), jnp.bfloat16),
            vector,
            jax.ShapeDtypeStruct((NBLOCK, 128), jnp.int32),
            vector,
        ],
        in_specs=[pl.BlockSpec(memory_space=pl.ANY)] + [hbm()] * 4,
        out_specs=[vmem()] * 4,
        scratch_shapes=[pltpu.VMEM((NBLOCK, NNZ, BLOCK, BLOCK), jnp.bfloat16), pltpu.SemaphoreType.DMA((PARTS + 3,))],
        cost_estimate=pl.CostEstimate(flops=0, bytes_accessed=11_000_000, transcendentals=0),
        **PARAMS,
    )(halo, *(in_hbm(a) for a in (blocks, speeds.reshape(NBLOCK, 128), upward.reshape(NBLOCK, 128), damping.reshape(NBLOCK, 128))))
    back = pl.pallas_call(
        steps_kernel,
        out_shape=msg_type,
        in_specs=[pl.BlockSpec(memory_space=pltpu.SMEM)] + [vmem()] * 7,
        out_specs=vmem(),
        scratch_shapes=[
            pltpu.VMEM((NBLOCK, 32, 128), jnp.float32),
            pltpu.VMEM((NBLOCK, 32, 128), jnp.bfloat16),
            pltpu.VMEM((NBLOCK, 32, 128), jnp.float32),
            pltpu.VMEM((NBLOCK, 16, 128), jnp.float32),
            pltpu.VMEM((NBLOCK, 16, 128), jnp.bfloat16),
        ],
        **PARAMS,
    )(jnp.transpose(block_cols), rec, low, high, *prepared)
    got = lax.all_to_all(back, PLANE, split_axis=0, concat_axis=0, tiled=True)
    out = pl.pallas_call(
        unpack_kernel, out_shape=jax.ShapeDtypeStruct((192, 256), jnp.float32), in_specs=[vmem()], out_specs=vmem(), **PARAMS
    )(got)
    return jnp.transpose(out).reshape(256, 1, 192)


def solution(mesh):
    fine = Mesh(mesh.devices.reshape(2, 4, 2, 32, 2), ("xh", "y", "core", "z", "xl"))
    return jax.shard_map(
        on_device,
        mesh=fine,
        in_specs=(P(MODE, ("z", "xl"), None), P(), P(), P(("z", "xl"), None), P(), P(), P()),
        out_specs=P(MODE, ("z", "xl"), None),
        check_vma=False,
    )
```

```python
import jax
import jax.numpy as jnp
from jax import lax
from jax.experimental import pallas as pl
from jax.experimental.pallas import tpu as pltpu
from jax.sharding import Mesh, PartitionSpec as P

MODE = ("xh", "y", "core")
PLANE = ("xh", "y", "core", "xl")
PEERS = 32
COLS = 6
NBLOCK = 32
NNZ = 5
BLOCK = 128
HALO_ROWS = 392
CHUNK = 4
PARTS = NBLOCK // CHUNK
RELAX = 0.25
VMEM_LIMIT = 32 * 1024 * 1024


def pack_kernel(x_hbm, c_hbm, msg_ref, x_ref, c_ref, sems):
    copies = [
        pltpu.make_async_copy(x_hbm, x_ref, sems.at[0]),
        pltpu.make_async_copy(c_hbm, c_ref, sems.at[1]),
    ]
    for copy in copies:
        copy.start()
    for copy in copies:
        copy.wait()
    for j in range(PEERS):
        for h in range(2):
            msg_ref[j, 8 * h : 8 * h + 6, :] = x_ref[COLS * j : COLS * j + 6, 128 * h : 128 * h + 128]
        msg_ref[j, 6:7, 0:6] = c_ref[0:1, COLS * j : COLS * j + 6]


def halo_kernel(rec_ref, out_ref):
    for d in range(16):
        for xl in range(2):
            for h in range(2):
                row = 24 * d + 12 * xl + 6 * h
                out_ref[row : row + 8, :] = rec_ref[2 * d + xl, 8 * h : 8 * h + 8, :]
    out_ref[384:385, :] = rec_ref[0, 6:7, :]
    out_ref[385:386, :] = rec_ref[1, 6:7, :]


def on_rows(row):
    lane = lax.broadcasted_iota(jnp.int32, (8, 128), 1)
    cell = lax.broadcasted_iota(jnp.int32, (8, 128), 0)
    picked = jnp.where(lane == cell, jnp.broadcast_to(row, (8, 128)), 0.0)
    return jnp.broadcast_to(jnp.sum(picked, axis=1, keepdims=True), (8, 128))


def prepare_kernel(
    _, blocks_hbm, speeds_hbm, upward_hbm, damping_hbm,
    turned_ref, speeds_ref, upward_ref, damping_ref, blocks_ref, sems,
):
    vectors = [
        pltpu.make_async_copy(speeds_hbm, speeds_ref, sems.at[PARTS]),
        pltpu.make_async_copy(upward_hbm, upward_ref, sems.at[PARTS + 1]),
        pltpu.make_async_copy(damping_hbm, damping_ref, sems.at[PARTS + 2]),
    ]
    copies = []
    for i in range(PARTS):
        part = pl.ds(CHUNK * i, CHUNK)
        copies.append(pltpu.make_async_copy(blocks_hbm.at[part], blocks_ref.at[part], sems.at[i]))
    for copy in copies + vectors:
        copy.start()
    for i in range(PARTS):
        copies[i].wait()
        for r in range(CHUNK * i, CHUNK * i + CHUNK):
            for k in range(NNZ):
                turned_ref[r, BLOCK * k : BLOCK * k + BLOCK, :] = blocks_ref[r, k].T
    for copy in vectors:
        copy.wait()


def steps_kernel(
    cols_ref, rec_ref, high_ref, low_ref, turned_ref, speeds_ref, upward_ref, damping_ref,
    out_ref, adv_ref, rounded_ref, adv2_ref, rounded2_ref,
):
    courant = [
        on_rows(low_ref[385:386, :]),
        on_rows(rec_ref[0, 6:7, :]),
        on_rows(rec_ref[1, 6:7, :]),
        on_rows(high_ref[384:385, :]),
    ]

    for b in range(NBLOCK):
        d, h = divmod(b, 2)
        row = 24 * d + 6 * h
        layers = [
            low_ref[row : row + 8, :],
            low_ref[row + 12 : row + 20, :],
            rec_ref[2 * d, 8 * h : 8 * h + 8, :],
            rec_ref[2 * d + 1, 8 * h : 8 * h + 8, :],
            high_ref[row : row + 8, :],
            high_ref[row + 12 : row + 20, :],
        ]
        speed = speeds_ref[b : b + 1, :]
        up = jnp.broadcast_to(upward_ref[b : b + 1, :], (8, 128)) == 1
        moved = []
        for k in range(4):
            here = layers[k + 1]
            chosen = jnp.where(up, layers[k], layers[k + 2])
            moved.append(here - courant[k] * speed * (here - chosen))
        moved = jnp.concatenate(moved, axis=0)
        adv_ref[b] = moved
        rounded_ref[b] = moved.astype(jnp.bfloat16)

    def sources(r, values_ref):
        rows = values_ref.shape[1]
        picked = [[values_ref[cols_ref[k, r + i]] for k in range(NNZ)] for i in range(2)]
        most = [
            jnp.dot(jnp.concatenate(picked[i][:4], axis=1), turned_ref[r + i, : 4 * BLOCK], preferred_element_type=jnp.float32)
            for i in range(2)
        ]
        none = jnp.zeros((rows, BLOCK), jnp.bfloat16)
        fifth = jnp.concatenate(
            [jnp.concatenate([picked[0][4], none], axis=1), jnp.concatenate([none, picked[1][4]], axis=1)], axis=0
        )
        stored = jnp.concatenate([turned_ref[r + i, 4 * BLOCK :] for i in range(2)], axis=0)
        rest = jnp.dot(fifth, stored, preferred_element_type=jnp.float32)
        return most[0] + rest[:rows], most[1] + rest[rows:]

    for r in range(0, NBLOCK, 2):
        for b, source in zip((r, r + 1), sources(r, rounded_ref)):
            adv = adv_ref[b]
            field = adv + RELAX * (source - damping_ref[b : b + 1, :] * adv * jnp.abs(adv))
            speed = speeds_ref[b : b + 1, :]
            up = jnp.broadcast_to(upward_ref[b : b + 1, :], (8, 128)) == 1
            moved = []
            for k in range(2):
                here = field[8 * k + 8 : 8 * k + 16]
                chosen = jnp.where(up, field[8 * k : 8 * k + 8], field[8 * k + 16 : 8 * k + 24])
                moved.append(here - courant[k + 1] * speed * (here - chosen))
            moved = jnp.concatenate(moved, axis=0)
            adv2_ref[b] = moved
            rounded2_ref[b] = moved.astype(jnp.bfloat16)

    for r in range(0, NBLOCK, 2):
        for b, source in zip((r, r + 1), sources(r, rounded2_ref)):
            d, h = divmod(b, 2)
            adv = adv2_ref[b]
            last = adv + RELAX * (source - damping_ref[b : b + 1, :] * adv * jnp.abs(adv))
            for k in range(2):
                tile = 3 * (2 * d + k)
                rows = last[8 * k : 8 * k + 6]
                if h == 0:
                    out_ref[tile] = rows[0:4]
                    out_ref[tile + 1, 0:2, :] = rows[4:6]
                else:
                    out_ref[tile + 1, 2:4, :] = rows[0:2]
                    out_ref[tile + 2] = rows[2:6]


def unpack_kernel(msg_ref, out_ref):
    for j in range(PEERS):
        row = COLS * j
        out_ref[row : row + 4, 0:128] = msg_ref[3 * j]
        out_ref[row + 4 : row + 6, 0:128] = msg_ref[3 * j + 1, 0:2, :]
        out_ref[row : row + 2, 128:256] = msg_ref[3 * j + 1, 2:4, :]
        out_ref[row + 2 : row + 6, 128:256] = msg_ref[3 * j + 2]


def vmem():
    return pl.BlockSpec(memory_space=pltpu.VMEM)


def hbm():
    return pl.BlockSpec(memory_space=pltpu.HBM)


def in_hbm(array):
    return pltpu.with_memory_space_constraint(array, pltpu.HBM)


PARAMS = dict(compiler_params=pltpu.CompilerParams(vmem_limit_bytes=VMEM_LIMIT))


def on_device(phonons, speeds, upward, courant, blocks, block_cols, damping):
    zs = lax.axis_size("z")
    up = [(i, i + 1) for i in range(zs - 1)]
    down = [(j, i) for i, j in up]
    cells = jnp.transpose(phonons.reshape(256, 192))
    msg_type = jax.ShapeDtypeStruct((PEERS, 16, 128), jnp.float32)

    msg = pl.pallas_call(
        pack_kernel,
        out_shape=msg_type,
        in_specs=[hbm()] * 2,
        out_specs=vmem(),
        scratch_shapes=[pltpu.VMEM((192, 256), jnp.float32), pltpu.VMEM((1, 192), jnp.float32), pltpu.SemaphoreType.DMA((2,))],
        **PARAMS,
    )(in_hbm(cells), in_hbm(courant))
    rec = lax.all_to_all(msg, PLANE, split_axis=0, concat_axis=0, tiled=True)
    halo = pl.pallas_call(
        halo_kernel, out_shape=jax.ShapeDtypeStruct((HALO_ROWS, 128), jnp.float32), in_specs=[vmem()], out_specs=vmem(), **PARAMS
    )(rec)
    low = lax.ppermute(halo, "z", up)
    high = lax.ppermute(halo, "z", down)
    vector = jax.ShapeDtypeStruct((NBLOCK, 128), jnp.float32)
    prepared = pl.pallas_call(
        prepare_kernel,
        out_shape=[
            jax.ShapeDtypeStruct((NBLOCK, NNZ * BLOCK, BLOCK), jnp.bfloat16),
            vector,
            jax.ShapeDtypeStruct((NBLOCK, 128), jnp.int32),
            vector,
        ],
        in_specs=[pl.BlockSpec(memory_space=pl.ANY)] + [hbm()] * 4,
        out_specs=[vmem()] * 4,
        scratch_shapes=[pltpu.VMEM((NBLOCK, NNZ, BLOCK, BLOCK), jnp.bfloat16), pltpu.SemaphoreType.DMA((PARTS + 3,))],
        cost_estimate=pl.CostEstimate(flops=0, bytes_accessed=11_000_000, transcendentals=0),
        **PARAMS,
    )(halo, *(in_hbm(a) for a in (blocks, speeds.reshape(NBLOCK, 128), upward.reshape(NBLOCK, 128), damping.reshape(NBLOCK, 128))))
    back = pl.pallas_call(
        steps_kernel,
        out_shape=jax.ShapeDtypeStruct((3 * PEERS, 4, 128), jnp.float32),
        in_specs=[pl.BlockSpec(memory_space=pltpu.SMEM)] + [vmem()] * 7,
        out_specs=vmem(),
        scratch_shapes=[
            pltpu.VMEM((NBLOCK, 32, 128), jnp.float32),
            pltpu.VMEM((NBLOCK, 32, 128), jnp.bfloat16),
            pltpu.VMEM((NBLOCK, 16, 128), jnp.float32),
            pltpu.VMEM((NBLOCK, 16, 128), jnp.bfloat16),
        ],
        **PARAMS,
    )(jnp.transpose(block_cols), rec, high, low, *prepared)
    got = lax.all_to_all(back, PLANE, split_axis=0, concat_axis=0, tiled=True)
    out = pl.pallas_call(
        unpack_kernel, out_shape=jax.ShapeDtypeStruct((192, 256), jnp.float32), in_specs=[vmem()], out_specs=vmem(), **PARAMS
    )(got)
    return jnp.transpose(out).reshape(256, 1, 192)


def solution(mesh):
    fine = Mesh(mesh.devices.reshape(2, 4, 2, 32, 2), ("xh", "y", "core", "z", "xl"))
    return jax.shard_map(
        on_device,
        mesh=fine,
        in_specs=(P(MODE, ("z", "xl"), None), P(), P(), P(("z", "xl"), None), P(), P(), P()),
        out_specs=P(MODE, ("z", "xl"), None),
        check_vma=False,
    )
```

```python
import jax
import jax.numpy as jnp
from jax import lax
from jax.experimental import pallas as pl
from jax.experimental.pallas import tpu as pltpu
from jax.sharding import Mesh, PartitionSpec as P

MODE = ("xh", "y", "core")
PLANE = ("xh", "y", "core", "xl")
PEERS = 32
COLS = 6
NBLOCK = 32
NNZ = 5
BLOCK = 128
HALO_ROWS = 392
CHUNK = 4
PARTS = NBLOCK // CHUNK
RELAX = 0.25
VMEM_LIMIT = 32 * 1024 * 1024


def pack_kernel(x_hbm, c_hbm, msg_ref, x_ref, c_ref, sems):
    copies = [
        pltpu.make_async_copy(x_hbm, x_ref, sems.at[0]),
        pltpu.make_async_copy(c_hbm, c_ref, sems.at[1]),
    ]
    for copy in copies:
        copy.start()
    for copy in copies:
        copy.wait()
    for j in range(PEERS):
        for h in range(2):
            msg_ref[j, 8 * h : 8 * h + 6, :] = x_ref[COLS * j : COLS * j + 6, 128 * h : 128 * h + 128]
        msg_ref[j, 6:7, 0:6] = c_ref[0:1, COLS * j : COLS * j + 6]


def halo_kernel(rec_ref, out_ref):
    for d in range(16):
        for xl in range(2):
            for h in range(2):
                row = 24 * d + 12 * xl + 6 * h
                out_ref[row : row + 8, :] = rec_ref[2 * d + xl, 8 * h : 8 * h + 8, :]
    out_ref[384:385, :] = rec_ref[0, 6:7, :]
    out_ref[385:386, :] = rec_ref[1, 6:7, :]


def on_rows(row):
    lane = lax.broadcasted_iota(jnp.int32, (8, 128), 1)
    cell = lax.broadcasted_iota(jnp.int32, (8, 128), 0)
    picked = jnp.where(lane == cell, jnp.broadcast_to(row, (8, 128)), 0.0)
    return jnp.broadcast_to(jnp.sum(picked, axis=1, keepdims=True), (8, 128))


def prepare_kernel(
    _, blocks_hbm, speeds_hbm, upward_hbm, damping_hbm,
    turned_ref, speeds_ref, upward_ref, damping_ref, blocks_ref, sems,
):
    vectors = [
        pltpu.make_async_copy(speeds_hbm, speeds_ref, sems.at[PARTS]),
        pltpu.make_async_copy(upward_hbm, upward_ref, sems.at[PARTS + 1]),
        pltpu.make_async_copy(damping_hbm, damping_ref, sems.at[PARTS + 2]),
    ]
    copies = []
    for i in range(PARTS):
        part = pl.ds(CHUNK * i, CHUNK)
        copies.append(pltpu.make_async_copy(blocks_hbm.at[part], blocks_ref.at[part], sems.at[i]))
    for copy in copies + vectors:
        copy.start()
    for i in range(PARTS):
        copies[i].wait()
        for r in range(CHUNK * i, CHUNK * i + CHUNK):
            for k in range(NNZ):
                turned_ref[r, BLOCK * k : BLOCK * k + BLOCK, :] = blocks_ref[r, k].T
    for copy in vectors:
        copy.wait()


def steps_kernel(
    cols_ref, rec_ref, even_ref, odd_ref, turned_ref, speeds_ref, upward_ref, damping_ref,
    out_ref, adv_ref, rounded_ref, adv2_ref, rounded2_ref,
):
    is_odd = lax.axis_index("z") % 2 == 1

    def low(row, rows):
        return jnp.where(is_odd, even_ref[row : row + rows, :], odd_ref[row : row + rows, :])

    def high(row, rows):
        return jnp.where(is_odd, odd_ref[row : row + rows, :], even_ref[row : row + rows, :])

    courant = [
        on_rows(low(385, 1)),
        on_rows(rec_ref[0, 6:7, :]),
        on_rows(rec_ref[1, 6:7, :]),
        on_rows(high(384, 1)),
    ]

    for b in range(NBLOCK):
        d, h = divmod(b, 2)
        row = 24 * d + 6 * h
        layers = [
            low(row, 8),
            low(row + 12, 8),
            rec_ref[2 * d, 8 * h : 8 * h + 8, :],
            rec_ref[2 * d + 1, 8 * h : 8 * h + 8, :],
            high(row, 8),
            high(row + 12, 8),
        ]
        speed = speeds_ref[b : b + 1, :]
        up = jnp.broadcast_to(upward_ref[b : b + 1, :], (8, 128)) == 1
        moved = []
        for k in range(4):
            here = layers[k + 1]
            chosen = jnp.where(up, layers[k], layers[k + 2])
            moved.append(here - courant[k] * speed * (here - chosen))
        moved = jnp.concatenate(moved, axis=0)
        adv_ref[b] = moved
        rounded_ref[b] = moved.astype(jnp.bfloat16)

    def sources(r, values_ref):
        rows = values_ref.shape[1]
        picked = [[values_ref[cols_ref[k, r + i]] for k in range(NNZ)] for i in range(2)]
        most = [
            jnp.dot(jnp.concatenate(picked[i][:4], axis=1), turned_ref[r + i, : 4 * BLOCK], preferred_element_type=jnp.float32)
            for i in range(2)
        ]
        none = jnp.zeros((rows, BLOCK), jnp.bfloat16)
        fifth = jnp.concatenate(
            [jnp.concatenate([picked[0][4], none], axis=1), jnp.concatenate([none, picked[1][4]], axis=1)], axis=0
        )
        stored = jnp.concatenate([turned_ref[r + i, 4 * BLOCK :] for i in range(2)], axis=0)
        rest = jnp.dot(fifth, stored, preferred_element_type=jnp.float32)
        return most[0] + rest[:rows], most[1] + rest[rows:]

    for r in range(0, NBLOCK, 2):
        for b, source in zip((r, r + 1), sources(r, rounded_ref)):
            adv = adv_ref[b]
            field = adv + RELAX * (source - damping_ref[b : b + 1, :] * adv * jnp.abs(adv))
            speed = speeds_ref[b : b + 1, :]
            up = jnp.broadcast_to(upward_ref[b : b + 1, :], (8, 128)) == 1
            moved = []
            for k in range(2):
                here = field[8 * k + 8 : 8 * k + 16]
                chosen = jnp.where(up, field[8 * k : 8 * k + 8], field[8 * k + 16 : 8 * k + 24])
                moved.append(here - courant[k + 1] * speed * (here - chosen))
            moved = jnp.concatenate(moved, axis=0)
            adv2_ref[b] = moved
            rounded2_ref[b] = moved.astype(jnp.bfloat16)

    for r in range(0, NBLOCK, 2):
        for b, source in zip((r, r + 1), sources(r, rounded2_ref)):
            d, h = divmod(b, 2)
            adv = adv2_ref[b]
            last = adv + RELAX * (source - damping_ref[b : b + 1, :] * adv * jnp.abs(adv))
            for k in range(2):
                tile = 3 * (2 * d + k)
                rows = last[8 * k : 8 * k + 6]
                if h == 0:
                    out_ref[tile] = rows[0:4]
                    out_ref[tile + 1, 0:2, :] = rows[4:6]
                else:
                    out_ref[tile + 1, 2:4, :] = rows[0:2]
                    out_ref[tile + 2] = rows[2:6]


def unpack_kernel(msg_ref, out_ref):
    for j in range(PEERS):
        row = COLS * j
        out_ref[row : row + 4, 0:128] = msg_ref[3 * j]
        out_ref[row + 4 : row + 6, 0:128] = msg_ref[3 * j + 1, 0:2, :]
        out_ref[row : row + 2, 128:256] = msg_ref[3 * j + 1, 2:4, :]
        out_ref[row + 2 : row + 6, 128:256] = msg_ref[3 * j + 2]


def vmem():
    return pl.BlockSpec(memory_space=pltpu.VMEM)


def hbm():
    return pl.BlockSpec(memory_space=pltpu.HBM)


def in_hbm(array):
    return pltpu.with_memory_space_constraint(array, pltpu.HBM)


PARAMS = dict(compiler_params=pltpu.CompilerParams(vmem_limit_bytes=VMEM_LIMIT))


def on_device(phonons, speeds, upward, courant, blocks, block_cols, damping):
    zs = lax.axis_size("z")
    even = [pair for i in range(0, zs - 1, 2) for pair in ((i, i + 1), (i + 1, i))]
    odd = [pair for i in range(1, zs - 1, 2) for pair in ((i, i + 1), (i + 1, i))]
    cells = jnp.transpose(phonons.reshape(256, 192))
    msg_type = jax.ShapeDtypeStruct((PEERS, 16, 128), jnp.float32)

    msg = pl.pallas_call(
        pack_kernel,
        out_shape=msg_type,
        in_specs=[hbm()] * 2,
        out_specs=vmem(),
        scratch_shapes=[pltpu.VMEM((192, 256), jnp.float32), pltpu.VMEM((1, 192), jnp.float32), pltpu.SemaphoreType.DMA((2,))],
        **PARAMS,
    )(in_hbm(cells), in_hbm(courant))
    rec = lax.all_to_all(msg, PLANE, split_axis=0, concat_axis=0, tiled=True)
    halo = pl.pallas_call(
        halo_kernel, out_shape=jax.ShapeDtypeStruct((HALO_ROWS, 128), jnp.float32), in_specs=[vmem()], out_specs=vmem(), **PARAMS
    )(rec)
    even_got = lax.ppermute(halo, "z", even)
    odd_got = lax.ppermute(halo, "z", odd)
    vector = jax.ShapeDtypeStruct((NBLOCK, 128), jnp.float32)
    prepared = pl.pallas_call(
        prepare_kernel,
        out_shape=[
            jax.ShapeDtypeStruct((NBLOCK, NNZ * BLOCK, BLOCK), jnp.bfloat16),
            vector,
            jax.ShapeDtypeStruct((NBLOCK, 128), jnp.int32),
            vector,
        ],
        in_specs=[pl.BlockSpec(memory_space=pl.ANY)] + [hbm()] * 4,
        out_specs=[vmem()] * 4,
        scratch_shapes=[pltpu.VMEM((NBLOCK, NNZ, BLOCK, BLOCK), jnp.bfloat16), pltpu.SemaphoreType.DMA((PARTS + 3,))],
        cost_estimate=pl.CostEstimate(flops=0, bytes_accessed=11_000_000, transcendentals=0),
        **PARAMS,
    )(halo, *(in_hbm(a) for a in (blocks, speeds.reshape(NBLOCK, 128), upward.reshape(NBLOCK, 128), damping.reshape(NBLOCK, 128))))
    back = pl.pallas_call(
        steps_kernel,
        out_shape=jax.ShapeDtypeStruct((3 * PEERS, 4, 128), jnp.float32),
        in_specs=[pl.BlockSpec(memory_space=pltpu.SMEM)] + [vmem()] * 7,
        out_specs=vmem(),
        scratch_shapes=[
            pltpu.VMEM((NBLOCK, 32, 128), jnp.float32),
            pltpu.VMEM((NBLOCK, 32, 128), jnp.bfloat16),
            pltpu.VMEM((NBLOCK, 16, 128), jnp.float32),
            pltpu.VMEM((NBLOCK, 16, 128), jnp.bfloat16),
        ],
        **PARAMS,
    )(jnp.transpose(block_cols), rec, even_got, odd_got, *prepared)
    got = lax.all_to_all(back, PLANE, split_axis=0, concat_axis=0, tiled=True)
    out = pl.pallas_call(
        unpack_kernel, out_shape=jax.ShapeDtypeStruct((192, 256), jnp.float32), in_specs=[vmem()], out_specs=vmem(), **PARAMS
    )(got)
    return jnp.transpose(out).reshape(256, 1, 192)


def solution(mesh):
    fine = Mesh(mesh.devices.reshape(2, 4, 2, 32, 2), ("xh", "y", "core", "z", "xl"))
    return jax.shard_map(
        on_device,
        mesh=fine,
        in_specs=(P(MODE, ("z", "xl"), None), P(), P(), P(("z", "xl"), None), P(), P(), P()),
        out_specs=P(MODE, ("z", "xl"), None),
        check_vma=False,
    )
```

```python
import jax
import jax.numpy as jnp
from jax import lax
from jax.experimental import pallas as pl
from jax.experimental.pallas import tpu as pltpu
from jax.sharding import Mesh, PartitionSpec as P

MODE = ("xh", "y", "core")
PLANE = ("xh", "y", "core", "xl")
PEERS = 32
PIECES = 4
COLS = 6
NBLOCK = 32
NNZ = 5
BLOCK = 128
HALO_ROWS = 392
CHUNK = 4
PARTS = NBLOCK // CHUNK
RELAX = 0.25
VMEM_LIMIT = 32 * 1024 * 1024


def pack_kernel(x_hbm, c_hbm, msg_ref, x_ref, c_ref, sems):
    each = PEERS // PIECES
    courant = pltpu.make_async_copy(c_hbm, c_ref, sems.at[PIECES])
    copies = []
    for i in range(PIECES):
        part = pl.ds(COLS * each * i, COLS * each)
        copies.append(pltpu.make_async_copy(x_hbm.at[part], x_ref.at[part], sems.at[i]))
    for copy in copies + [courant]:
        copy.start()
    for i in range(PIECES):
        copies[i].wait()
        for j in range(each * i, each * i + each):
            for h in range(2):
                msg_ref[j, 8 * h : 8 * h + 6, :] = x_ref[COLS * j : COLS * j + 6, 128 * h : 128 * h + 128]
    courant.wait()
    for j in range(PEERS):
        msg_ref[j, 6:7, 0:6] = c_ref[0:1, COLS * j : COLS * j + 6]


def halo_kernel(rec_ref, out_ref):
    for d in range(16):
        for xl in range(2):
            for h in range(2):
                row = 24 * d + 12 * xl + 6 * h
                out_ref[row : row + 8, :] = rec_ref[2 * d + xl, 8 * h : 8 * h + 8, :]
    out_ref[384:385, :] = rec_ref[0, 6:7, :]
    out_ref[385:386, :] = rec_ref[1, 6:7, :]


def on_rows(row):
    lane = lax.broadcasted_iota(jnp.int32, (8, 128), 1)
    cell = lax.broadcasted_iota(jnp.int32, (8, 128), 0)
    picked = jnp.where(lane == cell, jnp.broadcast_to(row, (8, 128)), 0.0)
    return jnp.broadcast_to(jnp.sum(picked, axis=1, keepdims=True), (8, 128))


def prepare_kernel(
    _, blocks_hbm, speeds_hbm, upward_hbm, damping_hbm,
    turned_ref, speeds_ref, upward_ref, damping_ref, blocks_ref, sems,
):
    vectors = [
        pltpu.make_async_copy(speeds_hbm, speeds_ref, sems.at[PARTS]),
        pltpu.make_async_copy(upward_hbm, upward_ref, sems.at[PARTS + 1]),
        pltpu.make_async_copy(damping_hbm, damping_ref, sems.at[PARTS + 2]),
    ]
    copies = []
    for i in range(PARTS):
        part = pl.ds(CHUNK * i, CHUNK)
        copies.append(pltpu.make_async_copy(blocks_hbm.at[part], blocks_ref.at[part], sems.at[i]))
    for copy in copies + vectors:
        copy.start()
    for i in range(PARTS):
        copies[i].wait()
        for r in range(CHUNK * i, CHUNK * i + CHUNK):
            for k in range(NNZ):
                turned_ref[r, BLOCK * k : BLOCK * k + BLOCK, :] = blocks_ref[r, k].T
    for copy in vectors:
        copy.wait()


def steps_kernel(
    cols_ref, rec_ref, odd_ref, even_ref, turned_ref, speeds_ref, upward_ref, damping_ref,
    out_ref, adv_ref, rounded_ref, adv2_ref, rounded2_ref,
):
    is_odd = lax.axis_index("z") % 2 == 1

    def low(row, rows):
        return jnp.where(is_odd, even_ref[row : row + rows, :], odd_ref[row : row + rows, :])

    def high(row, rows):
        return jnp.where(is_odd, odd_ref[row : row + rows, :], even_ref[row : row + rows, :])

    courant = [
        on_rows(low(385, 1)),
        on_rows(rec_ref[0, 6:7, :]),
        on_rows(rec_ref[1, 6:7, :]),
        on_rows(high(384, 1)),
    ]

    for b in range(NBLOCK):
        d, h = divmod(b, 2)
        row = 24 * d + 6 * h
        layers = [
            low(row, 8),
            low(row + 12, 8),
            rec_ref[2 * d, 8 * h : 8 * h + 8, :],
            rec_ref[2 * d + 1, 8 * h : 8 * h + 8, :],
            high(row, 8),
            high(row + 12, 8),
        ]
        speed = speeds_ref[b : b + 1, :]
        up = jnp.broadcast_to(upward_ref[b : b + 1, :], (8, 128)) == 1
        moved = []
        for k in range(4):
            here = layers[k + 1]
            chosen = jnp.where(up, layers[k], layers[k + 2])
            moved.append(here - courant[k] * speed * (here - chosen))
        moved = jnp.concatenate(moved, axis=0)
        adv_ref[b] = moved
        rounded_ref[b] = moved.astype(jnp.bfloat16)

    def sources(r, values_ref):
        rows = values_ref.shape[1]
        picked = [[values_ref[cols_ref[k, r + i]] for k in range(NNZ)] for i in range(2)]
        most = [
            jnp.dot(jnp.concatenate(picked[i][:4], axis=1), turned_ref[r + i, : 4 * BLOCK], preferred_element_type=jnp.float32)
            for i in range(2)
        ]
        none = jnp.zeros((rows, BLOCK), jnp.bfloat16)
        fifth = jnp.concatenate(
            [jnp.concatenate([picked[0][4], none], axis=1), jnp.concatenate([none, picked[1][4]], axis=1)], axis=0
        )
        stored = jnp.concatenate([turned_ref[r + i, 4 * BLOCK :] for i in range(2)], axis=0)
        rest = jnp.dot(fifth, stored, preferred_element_type=jnp.float32)
        return most[0] + rest[:rows], most[1] + rest[rows:]

    for r in range(0, NBLOCK, 2):
        for b, source in zip((r, r + 1), sources(r, rounded_ref)):
            adv = adv_ref[b]
            field = adv + RELAX * (source - damping_ref[b : b + 1, :] * adv * jnp.abs(adv))
            speed = speeds_ref[b : b + 1, :]
            up = jnp.broadcast_to(upward_ref[b : b + 1, :], (8, 128)) == 1
            moved = []
            for k in range(2):
                here = field[8 * k + 8 : 8 * k + 16]
                chosen = jnp.where(up, field[8 * k : 8 * k + 8], field[8 * k + 16 : 8 * k + 24])
                moved.append(here - courant[k + 1] * speed * (here - chosen))
            moved = jnp.concatenate(moved, axis=0)
            adv2_ref[b] = moved
            rounded2_ref[b] = moved.astype(jnp.bfloat16)

    for r in range(0, NBLOCK, 2):
        for b, source in zip((r, r + 1), sources(r, rounded2_ref)):
            d, h = divmod(b, 2)
            adv = adv2_ref[b]
            last = adv + RELAX * (source - damping_ref[b : b + 1, :] * adv * jnp.abs(adv))
            for k in range(2):
                tile = 3 * (2 * d + k)
                rows = last[8 * k : 8 * k + 6]
                if h == 0:
                    out_ref[tile] = rows[0:4]
                    out_ref[tile + 1, 0:2, :] = rows[4:6]
                else:
                    out_ref[tile + 1, 2:4, :] = rows[0:2]
                    out_ref[tile + 2] = rows[2:6]


def unpack_kernel(msg_ref, out_ref):
    for j in range(PEERS):
        row = COLS * j
        out_ref[row : row + 4, 0:128] = msg_ref[3 * j]
        out_ref[row + 4 : row + 6, 0:128] = msg_ref[3 * j + 1, 0:2, :]
        out_ref[row : row + 2, 128:256] = msg_ref[3 * j + 1, 2:4, :]
        out_ref[row + 2 : row + 6, 128:256] = msg_ref[3 * j + 2]


def vmem():
    return pl.BlockSpec(memory_space=pltpu.VMEM)


def hbm():
    return pl.BlockSpec(memory_space=pltpu.HBM)


def in_hbm(array):
    return pltpu.with_memory_space_constraint(array, pltpu.HBM)


PARAMS = dict(compiler_params=pltpu.CompilerParams(vmem_limit_bytes=VMEM_LIMIT))


def on_device(phonons, speeds, upward, courant, blocks, block_cols, damping):
    zs = lax.axis_size("z")
    even = [pair for i in range(0, zs - 1, 2) for pair in ((i, i + 1), (i + 1, i))]
    odd = [pair for i in range(1, zs - 1, 2) for pair in ((i, i + 1), (i + 1, i))]
    cells = jnp.transpose(phonons.reshape(256, 192))
    msg_type = jax.ShapeDtypeStruct((PEERS, 16, 128), jnp.float32)

    msg = pl.pallas_call(
        pack_kernel,
        out_shape=msg_type,
        in_specs=[hbm()] * 2,
        out_specs=vmem(),
        scratch_shapes=[pltpu.VMEM((192, 256), jnp.float32), pltpu.VMEM((1, 192), jnp.float32), pltpu.SemaphoreType.DMA((PIECES + 1,))],
        **PARAMS,
    )(in_hbm(cells), in_hbm(courant))
    rec = lax.all_to_all(msg, PLANE, split_axis=0, concat_axis=0, tiled=True)
    halo = pl.pallas_call(
        halo_kernel, out_shape=jax.ShapeDtypeStruct((HALO_ROWS, 128), jnp.float32), in_specs=[vmem()], out_specs=vmem(), **PARAMS
    )(rec)
    even_got = lax.ppermute(halo, "z", even)
    odd_got = lax.ppermute(halo, "z", odd)
    vector = jax.ShapeDtypeStruct((NBLOCK, 128), jnp.float32)
    prepared = pl.pallas_call(
        prepare_kernel,
        out_shape=[
            jax.ShapeDtypeStruct((NBLOCK, NNZ * BLOCK, BLOCK), jnp.bfloat16),
            vector,
            jax.ShapeDtypeStruct((NBLOCK, 128), jnp.int32),
            vector,
        ],
        in_specs=[pl.BlockSpec(memory_space=pl.ANY)] + [hbm()] * 4,
        out_specs=[vmem()] * 4,
        scratch_shapes=[pltpu.VMEM((NBLOCK, NNZ, BLOCK, BLOCK), jnp.bfloat16), pltpu.SemaphoreType.DMA((PARTS + 3,))],
        cost_estimate=pl.CostEstimate(flops=0, bytes_accessed=11_000_000, transcendentals=0),
        **PARAMS,
    )(halo, *(in_hbm(a) for a in (blocks, speeds.reshape(NBLOCK, 128), upward.reshape(NBLOCK, 128), damping.reshape(NBLOCK, 128))))
    back = pl.pallas_call(
        steps_kernel,
        out_shape=jax.ShapeDtypeStruct((3 * PEERS, 4, 128), jnp.float32),
        in_specs=[vmem()] * 8,
        out_specs=vmem(),
        scratch_shapes=[
            pltpu.VMEM((NBLOCK, 32, 128), jnp.float32),
            pltpu.VMEM((NBLOCK, 32, 128), jnp.bfloat16),
            pltpu.VMEM((NBLOCK, 16, 128), jnp.float32),
            pltpu.VMEM((NBLOCK, 16, 128), jnp.bfloat16),
        ],
        **PARAMS,
    )(jnp.transpose(block_cols), rec, odd_got, even_got, *prepared)
    got = lax.all_to_all(back, PLANE, split_axis=0, concat_axis=0, tiled=True)
    out = pl.pallas_call(
        unpack_kernel, out_shape=jax.ShapeDtypeStruct((192, 256), jnp.float32), in_specs=[vmem()], out_specs=vmem(), **PARAMS
    )(got)
    return jnp.transpose(out).reshape(256, 1, 192)


def solution(mesh):
    fine = Mesh(mesh.devices.reshape(2, 4, 2, 32, 2), ("xh", "y", "core", "z", "xl"))
    return jax.shard_map(
        on_device,
        mesh=fine,
        in_specs=(P(MODE, ("z", "xl"), None), P(), P(), P(("z", "xl"), None), P(), P(), P()),
        out_specs=P(MODE, ("z", "xl"), None),
        check_vma=False,
    )
```

```python
import jax
import jax.numpy as jnp
from jax import lax
from jax.experimental import pallas as pl
from jax.experimental.pallas import tpu as pltpu
from jax.sharding import Mesh, PartitionSpec as P

MODE = ("xh", "y", "core")
PLANE = ("xh", "y", "core", "xl")
PEERS = 32
PIECES = 4
COLS = 6
NBLOCK = 32
NNZ = 5
BLOCK = 128
HALO_ROWS = 392
CHUNK = 4
PARTS = NBLOCK // CHUNK
RELAX = 0.25
VMEM_LIMIT = 32 * 1024 * 1024


def pack_kernel(x_hbm, c_hbm, msg_ref, x_ref, c_ref, sems):
    each = PEERS // PIECES
    courant = pltpu.make_async_copy(c_hbm, c_ref, sems.at[PIECES])
    copies = []
    for i in range(PIECES):
        part = pl.ds(COLS * each * i, COLS * each)
        copies.append(pltpu.make_async_copy(x_hbm.at[part], x_ref.at[part], sems.at[i]))
    for copy in copies + [courant]:
        copy.start()
    for i in range(PIECES):
        copies[i].wait()
        for j in range(each * i, each * i + each):
            for h in range(2):
                msg_ref[j, 8 * h : 8 * h + 6, :] = x_ref[COLS * j : COLS * j + 6, 128 * h : 128 * h + 128]
    courant.wait()
    for j in range(PEERS):
        msg_ref[j, 6:7, 0:6] = c_ref[0:1, COLS * j : COLS * j + 6]


def halo_kernel(rec_ref, out_ref):
    for d in range(16):
        for xl in range(2):
            for h in range(2):
                row = 24 * d + 12 * xl + 6 * h
                out_ref[row : row + 8, :] = rec_ref[2 * d + xl, 8 * h : 8 * h + 8, :]
    out_ref[384:385, :] = rec_ref[0, 6:7, :]
    out_ref[385:386, :] = rec_ref[1, 6:7, :]


def on_rows(row):
    lane = lax.broadcasted_iota(jnp.int32, (8, 128), 1)
    cell = lax.broadcasted_iota(jnp.int32, (8, 128), 0)
    picked = jnp.where(lane == cell, jnp.broadcast_to(row, (8, 128)), 0.0)
    return jnp.broadcast_to(jnp.sum(picked, axis=1, keepdims=True), (8, 128))


def prepare_kernel(
    _, blocks_hbm, speeds_hbm, upward_hbm, damping_hbm,
    turned_ref, speeds_ref, upward_ref, damping_ref, blocks_ref, sems,
):
    vectors = [
        pltpu.make_async_copy(speeds_hbm, speeds_ref, sems.at[PARTS]),
        pltpu.make_async_copy(upward_hbm, upward_ref, sems.at[PARTS + 1]),
        pltpu.make_async_copy(damping_hbm, damping_ref, sems.at[PARTS + 2]),
    ]
    copies = []
    for i in range(PARTS):
        part = pl.ds(CHUNK * i, CHUNK)
        copies.append(pltpu.make_async_copy(blocks_hbm.at[part], blocks_ref.at[part], sems.at[i]))
    for copy in copies + vectors:
        copy.start()
    for i in range(PARTS):
        copies[i].wait()
        for r in range(CHUNK * i, CHUNK * i + CHUNK):
            for k in range(NNZ):
                turned_ref[r, BLOCK * k : BLOCK * k + BLOCK, :] = blocks_ref[r, k].T
    for copy in vectors:
        copy.wait()


def steps_kernel(
    cols_ref, rec_ref, even_ref, odd_ref, turned_ref, speeds_ref, upward_ref, damping_ref,
    out_ref, adv_ref, rounded_ref, adv2_ref, rounded2_ref,
):
    is_odd = lax.axis_index("z") % 2 == 1

    def low(row, rows):
        return jnp.where(is_odd, even_ref[row : row + rows, :], odd_ref[row : row + rows, :])

    def high(row, rows):
        return jnp.where(is_odd, odd_ref[row : row + rows, :], even_ref[row : row + rows, :])

    courant = [
        on_rows(low(385, 1)),
        on_rows(rec_ref[0, 6:7, :]),
        on_rows(rec_ref[1, 6:7, :]),
        on_rows(high(384, 1)),
    ]

    for b in range(NBLOCK):
        d, h = divmod(b, 2)
        row = 24 * d + 6 * h
        layers = [
            low(row, 8),
            low(row + 12, 8),
            rec_ref[2 * d, 8 * h : 8 * h + 8, :],
            rec_ref[2 * d + 1, 8 * h : 8 * h + 8, :],
            high(row, 8),
            high(row + 12, 8),
        ]
        speed = speeds_ref[b : b + 1, :]
        up = jnp.broadcast_to(upward_ref[b : b + 1, :], (8, 128)) == 1
        moved = []
        for k in range(4):
            here = layers[k + 1]
            chosen = jnp.where(up, layers[k], layers[k + 2])
            moved.append(here - courant[k] * speed * (here - chosen))
        moved = jnp.concatenate(moved, axis=0)
        adv_ref[b] = moved
        rounded_ref[b] = moved.astype(jnp.bfloat16)

    def sources(r, values_ref):
        rows = values_ref.shape[1]
        picked = [[values_ref[cols_ref[k, r + i]] for k in range(NNZ)] for i in range(2)]
        most = [
            jnp.dot(jnp.concatenate(picked[i][:4], axis=1), turned_ref[r + i, : 4 * BLOCK], preferred_element_type=jnp.float32)
            for i in range(2)
        ]
        none = jnp.zeros((rows, BLOCK), jnp.bfloat16)
        fifth = jnp.concatenate(
            [jnp.concatenate([picked[0][4], none], axis=1), jnp.concatenate([none, picked[1][4]], axis=1)], axis=0
        )
        stored = jnp.concatenate([turned_ref[r + i, 4 * BLOCK :] for i in range(2)], axis=0)
        rest = jnp.dot(fifth, stored, preferred_element_type=jnp.float32)
        return most[0] + rest[:rows], most[1] + rest[rows:]

    for r in range(0, NBLOCK, 2):
        for b, source in zip((r, r + 1), sources(r, rounded_ref)):
            adv = adv_ref[b]
            field = adv + RELAX * (source - damping_ref[b : b + 1, :] * adv * jnp.abs(adv))
            speed = speeds_ref[b : b + 1, :]
            up = jnp.broadcast_to(upward_ref[b : b + 1, :], (8, 128)) == 1
            moved = []
            for k in range(2):
                here = field[8 * k + 8 : 8 * k + 16]
                chosen = jnp.where(up, field[8 * k : 8 * k + 8], field[8 * k + 16 : 8 * k + 24])
                moved.append(here - courant[k + 1] * speed * (here - chosen))
            moved = jnp.concatenate(moved, axis=0)
            adv2_ref[b] = moved
            rounded2_ref[b] = moved.astype(jnp.bfloat16)

    for r in range(0, NBLOCK, 2):
        for b, source in zip((r, r + 1), sources(r, rounded2_ref)):
            d, h = divmod(b, 2)
            adv = adv2_ref[b]
            last = adv + RELAX * (source - damping_ref[b : b + 1, :] * adv * jnp.abs(adv))
            for k in range(2):
                tile = 3 * (2 * d + k)
                rows = last[8 * k : 8 * k + 6]
                if h == 0:
                    out_ref[tile] = rows[0:4]
                    out_ref[tile + 1, 0:2, :] = rows[4:6]
                else:
                    out_ref[tile + 1, 2:4, :] = rows[0:2]
                    out_ref[tile + 2] = rows[2:6]


def unpack_kernel(msg_ref, out_ref):
    for j in range(PEERS):
        row = COLS * j
        out_ref[row : row + 4, 0:128] = msg_ref[3 * j]
        out_ref[row + 4 : row + 6, 0:128] = msg_ref[3 * j + 1, 0:2, :]
        out_ref[row : row + 2, 128:256] = msg_ref[3 * j + 1, 2:4, :]
        out_ref[row + 2 : row + 6, 128:256] = msg_ref[3 * j + 2]


def vmem():
    return pl.BlockSpec(memory_space=pltpu.VMEM)


def hbm():
    return pl.BlockSpec(memory_space=pltpu.HBM)


def in_hbm(array):
    return pltpu.with_memory_space_constraint(array, pltpu.HBM)


PARAMS = dict(compiler_params=pltpu.CompilerParams(vmem_limit_bytes=VMEM_LIMIT))


def on_device(phonons, speeds, upward, courant, blocks, block_cols, damping):
    zs = lax.axis_size("z")
    even = [pair for i in range(0, zs - 1, 2) for pair in ((i, i + 1), (i + 1, i))]
    odd = [pair for i in range(1, zs - 1, 2) for pair in ((i, i + 1), (i + 1, i))]
    cells = jnp.transpose(phonons.reshape(256, 192))
    msg_type = jax.ShapeDtypeStruct((PEERS, 16, 128), jnp.float32)

    msg = pl.pallas_call(
        pack_kernel,
        out_shape=msg_type,
        in_specs=[hbm()] * 2,
        out_specs=vmem(),
        scratch_shapes=[pltpu.VMEM((192, 256), jnp.float32), pltpu.VMEM((1, 192), jnp.float32), pltpu.SemaphoreType.DMA((PIECES + 1,))],
        **PARAMS,
    )(in_hbm(cells), in_hbm(courant))
    rec = lax.all_to_all(msg, PLANE, split_axis=0, concat_axis=0, tiled=True)
    halo = pl.pallas_call(
        halo_kernel, out_shape=jax.ShapeDtypeStruct((HALO_ROWS, 128), jnp.float32), in_specs=[vmem()], out_specs=vmem(), **PARAMS
    )(rec)
    even_got = lax.ppermute(halo, "z", even)
    odd_got = lax.ppermute(halo, "z", odd)
    vector = jax.ShapeDtypeStruct((NBLOCK, 128), jnp.float32)
    prepared = pl.pallas_call(
        prepare_kernel,
        out_shape=[
            jax.ShapeDtypeStruct((NBLOCK, NNZ * BLOCK, BLOCK), jnp.bfloat16),
            vector,
            jax.ShapeDtypeStruct((NBLOCK, 128), jnp.int32),
            vector,
        ],
        in_specs=[pl.BlockSpec(memory_space=pl.ANY)] + [hbm()] * 4,
        out_specs=[vmem()] * 4,
        scratch_shapes=[pltpu.VMEM((NBLOCK, NNZ, BLOCK, BLOCK), jnp.bfloat16), pltpu.SemaphoreType.DMA((PARTS + 3,))],
        cost_estimate=pl.CostEstimate(flops=0, bytes_accessed=11_000_000, transcendentals=0),
        **PARAMS,
    )(halo, *(in_hbm(a) for a in (blocks, speeds.reshape(NBLOCK, 128), upward.reshape(NBLOCK, 128), damping.reshape(NBLOCK, 128))))
    back = pl.pallas_call(
        steps_kernel,
        out_shape=jax.ShapeDtypeStruct((3 * PEERS, 4, 128), jnp.float32),
        in_specs=[vmem()] * 8,
        out_specs=vmem(),
        scratch_shapes=[
            pltpu.VMEM((NBLOCK, 32, 128), jnp.float32),
            pltpu.VMEM((NBLOCK, 32, 128), jnp.bfloat16),
            pltpu.VMEM((NBLOCK, 16, 128), jnp.float32),
            pltpu.VMEM((NBLOCK, 16, 128), jnp.bfloat16),
        ],
        **PARAMS,
    )(jnp.transpose(block_cols), rec, even_got, odd_got, *prepared)
    got = lax.all_to_all(back, PLANE, split_axis=0, concat_axis=0, tiled=True)
    out = pl.pallas_call(
        unpack_kernel, out_shape=jax.ShapeDtypeStruct((192, 256), jnp.float32), in_specs=[vmem()], out_specs=vmem(), **PARAMS
    )(got)
    return jnp.transpose(out).reshape(256, 1, 192)


def solution(mesh):
    fine = Mesh(mesh.devices.reshape(2, 4, 2, 32, 2), ("xh", "y", "core", "z", "xl"))
    return jax.shard_map(
        on_device,
        mesh=fine,
        in_specs=(P(MODE, ("z", "xl"), None), P(), P(), P(("z", "xl"), None), P(), P(), P()),
        out_specs=P(MODE, ("z", "xl"), None),
        check_vma=False,
    )
```

```python
import jax
import jax.numpy as jnp
from jax import lax
from jax.experimental import pallas as pl
from jax.experimental.pallas import tpu as pltpu
from jax.sharding import Mesh, PartitionSpec as P

MODE = ("xh", "y", "core")
PLANE = ("xh", "y", "core", "xl")
PEERS = 32
UNITS = 7
PIECES = 4
COLS = 6
NBLOCK = 32
NNZ = 5
BLOCK = 128
HALO_ROWS = 392
CHUNK = 4
PARTS = NBLOCK // CHUNK
RELAX = 0.25
VMEM_LIMIT = 32 * 1024 * 1024


def pack_kernel(x_hbm, c_hbm, msg_ref, x_ref, c_ref, sems):
    each = PEERS // PIECES
    courant = pltpu.make_async_copy(c_hbm, c_ref, sems.at[PIECES])
    copies = []
    for i in range(PIECES):
        part = pl.ds(COLS * each * i, COLS * each)
        copies.append(pltpu.make_async_copy(x_hbm.at[part], x_ref.at[part], sems.at[i]))
    for copy in copies + [courant]:
        copy.start()
    for i in range(PIECES):
        copies[i].wait()
        for j in range(each * i, each * i + each):
            for h in range(2):
                for p in range(3):
                    row = COLS * j + 2 * p
                    msg_ref[UNITS * j + 3 * h + p] = x_ref[row : row + 2, 128 * h : 128 * h + 128]
    courant.wait()
    for j in range(PEERS):
        msg_ref[UNITS * j + 6, 0:1, 0:6] = c_ref[0:1, COLS * j : COLS * j + 6]


def halo_kernel(rec_ref, out_ref):
    for d in range(16):
        for xl in range(2):
            for h in range(2):
                for p in range(3):
                    row = 24 * d + 12 * xl + 6 * h + 2 * p
                    out_ref[row : row + 2, :] = rec_ref[UNITS * (2 * d + xl) + 3 * h + p]
    for xl in range(2):
        out_ref[384 + xl : 385 + xl, :] = rec_ref[UNITS * xl + 6, 0:1, :]


def on_rows(row):
    lane = lax.broadcasted_iota(jnp.int32, (8, 128), 1)
    cell = lax.broadcasted_iota(jnp.int32, (8, 128), 0)
    picked = jnp.where(lane == cell, jnp.broadcast_to(row, (8, 128)), 0.0)
    return jnp.broadcast_to(jnp.sum(picked, axis=1, keepdims=True), (8, 128))


def prepare_kernel(
    _, blocks_hbm, speeds_hbm, upward_hbm, damping_hbm,
    turned_ref, speeds_ref, upward_ref, damping_ref, blocks_ref, sems,
):
    vectors = [
        pltpu.make_async_copy(speeds_hbm, speeds_ref, sems.at[PARTS]),
        pltpu.make_async_copy(upward_hbm, upward_ref, sems.at[PARTS + 1]),
        pltpu.make_async_copy(damping_hbm, damping_ref, sems.at[PARTS + 2]),
    ]
    copies = []
    for i in range(PARTS):
        part = pl.ds(CHUNK * i, CHUNK)
        copies.append(pltpu.make_async_copy(blocks_hbm.at[part], blocks_ref.at[part], sems.at[i]))
    for copy in copies + vectors:
        copy.start()
    for i in range(PARTS):
        copies[i].wait()
        for r in range(CHUNK * i, CHUNK * i + CHUNK):
            for k in range(NNZ):
                turned_ref[r, BLOCK * k : BLOCK * k + BLOCK, :] = blocks_ref[r, k].T
    for copy in vectors:
        copy.wait()


def steps_kernel(
    cols_ref, own_ref, even_ref, odd_ref, turned_ref, speeds_ref, upward_ref, damping_ref,
    out_ref, adv_ref, rounded_ref, adv2_ref, rounded2_ref,
):
    is_odd = lax.axis_index("z") % 2 == 1

    def low(row, rows):
        return jnp.where(is_odd, even_ref[row : row + rows, :], odd_ref[row : row + rows, :])

    def high(row, rows):
        return jnp.where(is_odd, odd_ref[row : row + rows, :], even_ref[row : row + rows, :])

    courant = [
        on_rows(low(385, 1)),
        on_rows(own_ref[384:385, :]),
        on_rows(own_ref[385:386, :]),
        on_rows(high(384, 1)),
    ]

    for b in range(NBLOCK):
        d, h = divmod(b, 2)
        row = 24 * d + 6 * h
        layers = [
            low(row, 8),
            low(row + 12, 8),
            own_ref[row : row + 8, :],
            own_ref[row + 12 : row + 20, :],
            high(row, 8),
            high(row + 12, 8),
        ]
        speed = speeds_ref[b : b + 1, :]
        up = jnp.broadcast_to(upward_ref[b : b + 1, :], (8, 128)) == 1
        moved = []
        for k in range(4):
            here = layers[k + 1]
            chosen = jnp.where(up, layers[k], layers[k + 2])
            moved.append(here - courant[k] * speed * (here - chosen))
        moved = jnp.concatenate(moved, axis=0)
        adv_ref[b] = moved
        rounded_ref[b] = moved.astype(jnp.bfloat16)

    def sources(r, values_ref):
        rows = values_ref.shape[1]
        picked = [[values_ref[cols_ref[k, r + i]] for k in range(NNZ)] for i in range(2)]
        most = [
            jnp.dot(jnp.concatenate(picked[i][:4], axis=1), turned_ref[r + i, : 4 * BLOCK], preferred_element_type=jnp.float32)
            for i in range(2)
        ]
        none = jnp.zeros((rows, BLOCK), jnp.bfloat16)
        fifth = jnp.concatenate(
            [jnp.concatenate([picked[0][4], none], axis=1), jnp.concatenate([none, picked[1][4]], axis=1)], axis=0
        )
        stored = jnp.concatenate([turned_ref[r + i, 4 * BLOCK :] for i in range(2)], axis=0)
        rest = jnp.dot(fifth, stored, preferred_element_type=jnp.float32)
        return most[0] + rest[:rows], most[1] + rest[rows:]

    for r in range(0, NBLOCK, 2):
        for b, source in zip((r, r + 1), sources(r, rounded_ref)):
            adv = adv_ref[b]
            field = adv + RELAX * (source - damping_ref[b : b + 1, :] * adv * jnp.abs(adv))
            speed = speeds_ref[b : b + 1, :]
            up = jnp.broadcast_to(upward_ref[b : b + 1, :], (8, 128)) == 1
            moved = []
            for k in range(2):
                here = field[8 * k + 8 : 8 * k + 16]
                chosen = jnp.where(up, field[8 * k : 8 * k + 8], field[8 * k + 16 : 8 * k + 24])
                moved.append(here - courant[k + 1] * speed * (here - chosen))
            moved = jnp.concatenate(moved, axis=0)
            adv2_ref[b] = moved
            rounded2_ref[b] = moved.astype(jnp.bfloat16)

    for r in range(0, NBLOCK, 2):
        for b, source in zip((r, r + 1), sources(r, rounded2_ref)):
            d, h = divmod(b, 2)
            adv = adv2_ref[b]
            last = adv + RELAX * (source - damping_ref[b : b + 1, :] * adv * jnp.abs(adv))
            for k in range(2):
                tile = 3 * (2 * d + k)
                rows = last[8 * k : 8 * k + 6]
                if h == 0:
                    out_ref[tile] = rows[0:4]
                    out_ref[tile + 1, 0:2, :] = rows[4:6]
                else:
                    out_ref[tile + 1, 2:4, :] = rows[0:2]
                    out_ref[tile + 2] = rows[2:6]


def unpack_kernel(msg_ref, out_ref):
    for j in range(PEERS):
        row = COLS * j
        out_ref[row : row + 4, 0:128] = msg_ref[3 * j]
        out_ref[row + 4 : row + 6, 0:128] = msg_ref[3 * j + 1, 0:2, :]
        out_ref[row : row + 2, 128:256] = msg_ref[3 * j + 1, 2:4, :]
        out_ref[row + 2 : row + 6, 128:256] = msg_ref[3 * j + 2]


def vmem():
    return pl.BlockSpec(memory_space=pltpu.VMEM)


def hbm():
    return pl.BlockSpec(memory_space=pltpu.HBM)


def in_hbm(array):
    return pltpu.with_memory_space_constraint(array, pltpu.HBM)


PARAMS = dict(compiler_params=pltpu.CompilerParams(vmem_limit_bytes=VMEM_LIMIT))


def on_device(phonons, speeds, upward, courant, blocks, block_cols, damping):
    zs = lax.axis_size("z")
    even = [pair for i in range(0, zs - 1, 2) for pair in ((i, i + 1), (i + 1, i))]
    odd = [pair for i in range(1, zs - 1, 2) for pair in ((i, i + 1), (i + 1, i))]
    cells = jnp.transpose(phonons.reshape(256, 192))
    msg_type = jax.ShapeDtypeStruct((UNITS * PEERS, 2, 128), jnp.float32)

    msg = pl.pallas_call(
        pack_kernel,
        out_shape=msg_type,
        in_specs=[hbm()] * 2,
        out_specs=vmem(),
        scratch_shapes=[pltpu.VMEM((192, 256), jnp.float32), pltpu.VMEM((1, 192), jnp.float32), pltpu.SemaphoreType.DMA((PIECES + 1,))],
        **PARAMS,
    )(in_hbm(cells), in_hbm(courant))
    rec = lax.all_to_all(msg, PLANE, split_axis=0, concat_axis=0, tiled=True)
    halo = pl.pallas_call(
        halo_kernel, out_shape=jax.ShapeDtypeStruct((HALO_ROWS, 128), jnp.float32), in_specs=[vmem()], out_specs=vmem(), **PARAMS
    )(rec)
    even_got = lax.ppermute(halo, "z", even)
    odd_got = lax.ppermute(halo, "z", odd)
    vector = jax.ShapeDtypeStruct((NBLOCK, 128), jnp.float32)
    prepared = pl.pallas_call(
        prepare_kernel,
        out_shape=[
            jax.ShapeDtypeStruct((NBLOCK, NNZ * BLOCK, BLOCK), jnp.bfloat16),
            vector,
            jax.ShapeDtypeStruct((NBLOCK, 128), jnp.int32),
            vector,
        ],
        in_specs=[pl.BlockSpec(memory_space=pl.ANY)] + [hbm()] * 4,
        out_specs=[vmem()] * 4,
        scratch_shapes=[pltpu.VMEM((NBLOCK, NNZ, BLOCK, BLOCK), jnp.bfloat16), pltpu.SemaphoreType.DMA((PARTS + 3,))],
        cost_estimate=pl.CostEstimate(flops=0, bytes_accessed=11_000_000, transcendentals=0),
        **PARAMS,
    )(halo, *(in_hbm(a) for a in (blocks, speeds.reshape(NBLOCK, 128), upward.reshape(NBLOCK, 128), damping.reshape(NBLOCK, 128))))
    back = pl.pallas_call(
        steps_kernel,
        out_shape=jax.ShapeDtypeStruct((3 * PEERS, 4, 128), jnp.float32),
        in_specs=[vmem()] * 8,
        out_specs=vmem(),
        scratch_shapes=[
            pltpu.VMEM((NBLOCK, 32, 128), jnp.float32),
            pltpu.VMEM((NBLOCK, 32, 128), jnp.bfloat16),
            pltpu.VMEM((NBLOCK, 16, 128), jnp.float32),
            pltpu.VMEM((NBLOCK, 16, 128), jnp.bfloat16),
        ],
        **PARAMS,
    )(jnp.transpose(block_cols), halo, even_got, odd_got, *prepared)
    got = lax.all_to_all(back, PLANE, split_axis=0, concat_axis=0, tiled=True)
    out = pl.pallas_call(
        unpack_kernel, out_shape=jax.ShapeDtypeStruct((192, 256), jnp.float32), in_specs=[vmem()], out_specs=vmem(), **PARAMS
    )(got)
    return jnp.transpose(out).reshape(256, 1, 192)


def solution(mesh):
    fine = Mesh(mesh.devices.reshape(2, 4, 2, 32, 2), ("xh", "y", "core", "z", "xl"))
    return jax.shard_map(
        on_device,
        mesh=fine,
        in_specs=(P(MODE, ("z", "xl"), None), P(), P(), P(("z", "xl"), None), P(), P(), P()),
        out_specs=P(MODE, ("z", "xl"), None),
        check_vma=False,
    )
```

```python
import jax
import jax.numpy as jnp
from jax import lax
from jax.experimental import pallas as pl
from jax.experimental.pallas import tpu as pltpu
from jax.sharding import Mesh, PartitionSpec as P

MODE = ("xh", "y", "core")
PLANE = ("xl", "xh", "y", "core")
PEERS = 32
UNITS = 7
PIECES = 4
COLS = 6
NBLOCK = 32
NNZ = 5
BLOCK = 128
HALO_ROWS = 392
CHUNK = 4
PARTS = NBLOCK // CHUNK
RELAX = 0.25
VMEM_LIMIT = 32 * 1024 * 1024


def pack_kernel(x_hbm, c_hbm, msg_ref, x_ref, c_ref, sems):
    each = PEERS // PIECES
    courant = pltpu.make_async_copy(c_hbm, c_ref, sems.at[PIECES])
    copies = []
    for i in range(PIECES):
        part = pl.ds(COLS * each * i, COLS * each)
        copies.append(pltpu.make_async_copy(x_hbm.at[part], x_ref.at[part], sems.at[i]))
    for copy in copies + [courant]:
        copy.start()
    for i in range(PIECES):
        copies[i].wait()
        for j in range(each * i, each * i + each):
            for h in range(2):
                for p in range(3):
                    row = COLS * j + 2 * p
                    msg_ref[UNITS * j + 3 * h + p] = x_ref[row : row + 2, 128 * h : 128 * h + 128]
    courant.wait()
    for j in range(PEERS):
        msg_ref[UNITS * j + 6, 0:1, 0:6] = c_ref[0:1, COLS * j : COLS * j + 6]


def halo_kernel(rec_ref, out_ref):
    for d in range(16):
        for xl in range(2):
            for h in range(2):
                for p in range(3):
                    row = 24 * d + 12 * xl + 6 * h + 2 * p
                    out_ref[row : row + 2, :] = rec_ref[UNITS * (16 * xl + d) + 3 * h + p]
    for xl in range(2):
        out_ref[384 + xl : 385 + xl, :] = rec_ref[UNITS * 16 * xl + 6, 0:1, :]


def on_rows(row):
    lane = lax.broadcasted_iota(jnp.int32, (8, 128), 1)
    cell = lax.broadcasted_iota(jnp.int32, (8, 128), 0)
    picked = jnp.where(lane == cell, jnp.broadcast_to(row, (8, 128)), 0.0)
    return jnp.broadcast_to(jnp.sum(picked, axis=1, keepdims=True), (8, 128))


def prepare_kernel(
    _, blocks_hbm, speeds_hbm, upward_hbm, damping_hbm,
    turned_ref, speeds_ref, upward_ref, damping_ref, blocks_ref, sems,
):
    vectors = [
        pltpu.make_async_copy(speeds_hbm, speeds_ref, sems.at[PARTS]),
        pltpu.make_async_copy(upward_hbm, upward_ref, sems.at[PARTS + 1]),
        pltpu.make_async_copy(damping_hbm, damping_ref, sems.at[PARTS + 2]),
    ]
    copies = []
    for i in range(PARTS):
        part = pl.ds(CHUNK * i, CHUNK)
        copies.append(pltpu.make_async_copy(blocks_hbm.at[part], blocks_ref.at[part], sems.at[i]))
    for copy in copies + vectors:
        copy.start()
    for i in range(PARTS):
        copies[i].wait()
        for r in range(CHUNK * i, CHUNK * i + CHUNK):
            for k in range(NNZ):
                turned_ref[r, BLOCK * k : BLOCK * k + BLOCK, :] = blocks_ref[r, k].T
    for copy in vectors:
        copy.wait()


def steps_kernel(
    cols_ref, own_ref, even_ref, odd_ref, turned_ref, speeds_ref, upward_ref, damping_ref,
    out_ref, adv_ref, rounded_ref, adv2_ref, rounded2_ref,
):
    is_odd = lax.axis_index("z") % 2 == 1

    def low(row, rows):
        return jnp.where(is_odd, even_ref[row : row + rows, :], odd_ref[row : row + rows, :])

    def high(row, rows):
        return jnp.where(is_odd, odd_ref[row : row + rows, :], even_ref[row : row + rows, :])

    courant = [
        on_rows(low(385, 1)),
        on_rows(own_ref[384:385, :]),
        on_rows(own_ref[385:386, :]),
        on_rows(high(384, 1)),
    ]

    for b in range(NBLOCK):
        d, h = divmod(b, 2)
        row = 24 * d + 6 * h
        layers = [
            low(row, 8),
            low(row + 12, 8),
            own_ref[row : row + 8, :],
            own_ref[row + 12 : row + 20, :],
            high(row, 8),
            high(row + 12, 8),
        ]
        speed = speeds_ref[b : b + 1, :]
        up = jnp.broadcast_to(upward_ref[b : b + 1, :], (8, 128)) == 1
        moved = []
        for k in range(4):
            here = layers[k + 1]
            chosen = jnp.where(up, layers[k], layers[k + 2])
            moved.append(here - courant[k] * speed * (here - chosen))
        moved = jnp.concatenate(moved, axis=0)
        adv_ref[b] = moved
        rounded_ref[b] = moved.astype(jnp.bfloat16)

    def sources(r, values_ref):
        rows = values_ref.shape[1]
        picked = [[values_ref[cols_ref[k, r + i]] for k in range(NNZ)] for i in range(2)]
        most = [
            jnp.dot(jnp.concatenate(picked[i][:4], axis=1), turned_ref[r + i, : 4 * BLOCK], preferred_element_type=jnp.float32)
            for i in range(2)
        ]
        none = jnp.zeros((rows, BLOCK), jnp.bfloat16)
        fifth = jnp.concatenate(
            [jnp.concatenate([picked[0][4], none], axis=1), jnp.concatenate([none, picked[1][4]], axis=1)], axis=0
        )
        stored = jnp.concatenate([turned_ref[r + i, 4 * BLOCK :] for i in range(2)], axis=0)
        rest = jnp.dot(fifth, stored, preferred_element_type=jnp.float32)
        return most[0] + rest[:rows], most[1] + rest[rows:]

    for r in range(0, NBLOCK, 2):
        for b, source in zip((r, r + 1), sources(r, rounded_ref)):
            adv = adv_ref[b]
            field = adv + RELAX * (source - damping_ref[b : b + 1, :] * adv * jnp.abs(adv))
            speed = speeds_ref[b : b + 1, :]
            up = jnp.broadcast_to(upward_ref[b : b + 1, :], (8, 128)) == 1
            moved = []
            for k in range(2):
                here = field[8 * k + 8 : 8 * k + 16]
                chosen = jnp.where(up, field[8 * k : 8 * k + 8], field[8 * k + 16 : 8 * k + 24])
                moved.append(here - courant[k + 1] * speed * (here - chosen))
            moved = jnp.concatenate(moved, axis=0)
            adv2_ref[b] = moved
            rounded2_ref[b] = moved.astype(jnp.bfloat16)

    for r in range(0, NBLOCK, 2):
        for b, source in zip((r, r + 1), sources(r, rounded2_ref)):
            d, h = divmod(b, 2)
            adv = adv2_ref[b]
            last = adv + RELAX * (source - damping_ref[b : b + 1, :] * adv * jnp.abs(adv))
            for k in range(2):
                tile = 3 * (16 * k + d)
                rows = last[8 * k : 8 * k + 6]
                if h == 0:
                    out_ref[tile] = rows[0:4]
                    out_ref[tile + 1, 0:2, :] = rows[4:6]
                else:
                    out_ref[tile + 1, 2:4, :] = rows[0:2]
                    out_ref[tile + 2] = rows[2:6]


def unpack_kernel(msg_ref, out_hbm, out_ref, sems):
    each = PEERS // PIECES
    copies = []
    for i in range(PIECES):
        for j in range(each * i, each * i + each):
            row = COLS * j
            out_ref[row : row + 4, 0:128] = msg_ref[3 * j]
            out_ref[row + 4 : row + 6, 0:128] = msg_ref[3 * j + 1, 0:2, :]
            out_ref[row : row + 2, 128:256] = msg_ref[3 * j + 1, 2:4, :]
            out_ref[row + 2 : row + 6, 128:256] = msg_ref[3 * j + 2]
        part = pl.ds(COLS * each * i, COLS * each)
        copies.append(pltpu.make_async_copy(out_ref.at[part], out_hbm.at[part], sems.at[i]))
        copies[i].start()
    for copy in copies:
        copy.wait()


def vmem():
    return pl.BlockSpec(memory_space=pltpu.VMEM)


def hbm():
    return pl.BlockSpec(memory_space=pltpu.HBM)


def in_hbm(array):
    return pltpu.with_memory_space_constraint(array, pltpu.HBM)


PARAMS = dict(compiler_params=pltpu.CompilerParams(vmem_limit_bytes=VMEM_LIMIT))


def on_device(phonons, speeds, upward, courant, blocks, block_cols, damping):
    zs = lax.axis_size("z")
    even = [pair for i in range(0, zs - 1, 2) for pair in ((i, i + 1), (i + 1, i))]
    odd = [pair for i in range(1, zs - 1, 2) for pair in ((i, i + 1), (i + 1, i))]
    cells = jnp.transpose(phonons.reshape(256, 192))
    msg_type = jax.ShapeDtypeStruct((UNITS * PEERS, 2, 128), jnp.float32)

    msg = pl.pallas_call(
        pack_kernel,
        out_shape=msg_type,
        in_specs=[hbm()] * 2,
        out_specs=vmem(),
        scratch_shapes=[pltpu.VMEM((192, 256), jnp.float32), pltpu.VMEM((1, 192), jnp.float32), pltpu.SemaphoreType.DMA((PIECES + 1,))],
        **PARAMS,
    )(in_hbm(cells), in_hbm(courant))
    rec = lax.all_to_all(msg, PLANE, split_axis=0, concat_axis=0, tiled=True)
    halo = pl.pallas_call(
        halo_kernel, out_shape=jax.ShapeDtypeStruct((HALO_ROWS, 128), jnp.float32), in_specs=[vmem()], out_specs=vmem(), **PARAMS
    )(rec)
    even_got = lax.ppermute(halo, "z", even)
    odd_got = lax.ppermute(halo, "z", odd)
    vector = jax.ShapeDtypeStruct((NBLOCK, 128), jnp.float32)
    prepared = pl.pallas_call(
        prepare_kernel,
        out_shape=[
            jax.ShapeDtypeStruct((NBLOCK, NNZ * BLOCK, BLOCK), jnp.bfloat16),
            vector,
            jax.ShapeDtypeStruct((NBLOCK, 128), jnp.int32),
            vector,
        ],
        in_specs=[pl.BlockSpec(memory_space=pl.ANY)] + [hbm()] * 4,
        out_specs=[vmem()] * 4,
        scratch_shapes=[pltpu.VMEM((NBLOCK, NNZ, BLOCK, BLOCK), jnp.bfloat16), pltpu.SemaphoreType.DMA((PARTS + 3,))],
        cost_estimate=pl.CostEstimate(flops=0, bytes_accessed=11_000_000, transcendentals=0),
        **PARAMS,
    )(halo, *(in_hbm(a) for a in (blocks, speeds.reshape(NBLOCK, 128), upward.reshape(NBLOCK, 128), damping.reshape(NBLOCK, 128))))
    back = pl.pallas_call(
        steps_kernel,
        out_shape=jax.ShapeDtypeStruct((3 * PEERS, 4, 128), jnp.float32),
        in_specs=[vmem()] * 8,
        out_specs=vmem(),
        scratch_shapes=[
            pltpu.VMEM((NBLOCK, 32, 128), jnp.float32),
            pltpu.VMEM((NBLOCK, 32, 128), jnp.bfloat16),
            pltpu.VMEM((NBLOCK, 16, 128), jnp.float32),
            pltpu.VMEM((NBLOCK, 16, 128), jnp.bfloat16),
        ],
        **PARAMS,
    )(jnp.transpose(block_cols), halo, even_got, odd_got, *prepared)
    got = lax.all_to_all(back, PLANE, split_axis=0, concat_axis=0, tiled=True)
    out = pl.pallas_call(
        unpack_kernel,
        out_shape=jax.ShapeDtypeStruct((192, 256), jnp.float32),
        in_specs=[vmem()],
        out_specs=hbm(),
        scratch_shapes=[pltpu.VMEM((192, 256), jnp.float32), pltpu.SemaphoreType.DMA((PIECES,))],
        **PARAMS,
    )(got)
    return jnp.transpose(out).reshape(256, 1, 192)


def solution(mesh):
    fine = Mesh(mesh.devices.reshape(2, 4, 2, 32, 2), ("xh", "y", "core", "z", "xl"))
    return jax.shard_map(
        on_device,
        mesh=fine,
        in_specs=(P(MODE, ("z", "xl"), None), P(), P(), P(("z", "xl"), None), P(), P(), P()),
        out_specs=P(MODE, ("z", "xl"), None),
        check_vma=False,
    )
```

```python
import jax
import jax.numpy as jnp
from jax import lax
from jax.experimental import pallas as pl
from jax.experimental.pallas import tpu as pltpu
from jax.sharding import Mesh, PartitionSpec as P

MODE = ("xh", "y", "core")
PLANE = ("xh", "y", "core", "xl")
PEERS = 32
UNITS = 7
PIECES = 4
COLS = 6
NBLOCK = 32
NNZ = 5
BLOCK = 128
HALO_ROWS = 392
CHUNK = 4
PARTS = NBLOCK // CHUNK
RELAX = 0.25
VMEM_LIMIT = 32 * 1024 * 1024


def pack_kernel(x_hbm, c_hbm, msg_ref, x_ref, c_ref, sems):
    each = PEERS // PIECES
    courant = pltpu.make_async_copy(c_hbm, c_ref, sems.at[PIECES])
    copies = []
    for i in range(PIECES):
        part = pl.ds(COLS * each * i, COLS * each)
        copies.append(pltpu.make_async_copy(x_hbm.at[part], x_ref.at[part], sems.at[i]))
    for copy in copies + [courant]:
        copy.start()
    for i in range(PIECES):
        copies[i].wait()
        for j in range(each * i, each * i + each):
            for h in range(2):
                for p in range(3):
                    row = COLS * j + 2 * p
                    msg_ref[UNITS * j + 3 * h + p] = x_ref[row : row + 2, 128 * h : 128 * h + 128]
    courant.wait()
    for j in range(PEERS):
        msg_ref[UNITS * j + 6, 0:1, 0:6] = c_ref[0:1, COLS * j : COLS * j + 6]


def halo_kernel(rec_ref, out_ref):
    for d in range(16):
        for xl in range(2):
            for h in range(2):
                for p in range(3):
                    row = 24 * d + 12 * xl + 6 * h + 2 * p
                    out_ref[row : row + 2, :] = rec_ref[UNITS * (2 * d + xl) + 3 * h + p]
    for xl in range(2):
        out_ref[384 + xl : 385 + xl, :] = rec_ref[UNITS * xl + 6, 0:1, :]


def on_rows(row):
    lane = lax.broadcasted_iota(jnp.int32, (8, 128), 1)
    cell = lax.broadcasted_iota(jnp.int32, (8, 128), 0)
    picked = jnp.where(lane == cell, jnp.broadcast_to(row, (8, 128)), 0.0)
    return jnp.broadcast_to(jnp.sum(picked, axis=1, keepdims=True), (8, 128))


def prepare_kernel(
    _, blocks_hbm, speeds_hbm, upward_hbm, damping_hbm,
    turned_ref, speeds_ref, upward_ref, damping_ref, blocks_ref, sems,
):
    vectors = [
        pltpu.make_async_copy(speeds_hbm, speeds_ref, sems.at[PARTS]),
        pltpu.make_async_copy(upward_hbm, upward_ref, sems.at[PARTS + 1]),
        pltpu.make_async_copy(damping_hbm, damping_ref, sems.at[PARTS + 2]),
    ]
    copies = []
    for i in range(PARTS):
        part = pl.ds(CHUNK * i, CHUNK)
        copies.append(pltpu.make_async_copy(blocks_hbm.at[part], blocks_ref.at[part], sems.at[i]))
    for copy in copies + vectors:
        copy.start()
    for i in range(PARTS):
        copies[i].wait()
        for r in range(CHUNK * i, CHUNK * i + CHUNK):
            for k in range(NNZ):
                turned_ref[r, BLOCK * k : BLOCK * k + BLOCK, :] = blocks_ref[r, k].T
    for copy in vectors:
        copy.wait()


def steps_kernel(
    cols_ref, own_ref, even_ref, odd_ref, turned_ref, speeds_ref, upward_ref, damping_ref,
    out_ref, adv_ref, rounded_ref, adv2_ref, rounded2_ref,
):
    is_odd = lax.axis_index("z") % 2 == 1

    def low(row, rows):
        return jnp.where(is_odd, even_ref[row : row + rows, :], odd_ref[row : row + rows, :])

    def high(row, rows):
        return jnp.where(is_odd, odd_ref[row : row + rows, :], even_ref[row : row + rows, :])

    courant = [
        on_rows(low(385, 1)),
        on_rows(own_ref[384:385, :]),
        on_rows(own_ref[385:386, :]),
        on_rows(high(384, 1)),
    ]

    for b in range(NBLOCK):
        d, h = divmod(b, 2)
        row = 24 * d + 6 * h
        layers = [
            low(row, 8),
            low(row + 12, 8),
            own_ref[row : row + 8, :],
            own_ref[row + 12 : row + 20, :],
            high(row, 8),
            high(row + 12, 8),
        ]
        speed = speeds_ref[b : b + 1, :]
        up = jnp.broadcast_to(upward_ref[b : b + 1, :], (8, 128)) == 1
        moved = []
        for k in range(4):
            here = layers[k + 1]
            chosen = jnp.where(up, layers[k], layers[k + 2])
            moved.append(here - courant[k] * speed * (here - chosen))
        moved = jnp.concatenate(moved, axis=0)
        adv_ref[b] = moved
        rounded_ref[b] = moved.astype(jnp.bfloat16)

    def sources(r, values_ref):
        rows = values_ref.shape[1]
        picked = [[values_ref[cols_ref[k, r + i]] for k in range(NNZ)] for i in range(2)]
        most = [
            jnp.dot(jnp.concatenate(picked[i][:4], axis=1), turned_ref[r + i, : 4 * BLOCK], preferred_element_type=jnp.float32)
            for i in range(2)
        ]
        none = jnp.zeros((rows, BLOCK), jnp.bfloat16)
        fifth = jnp.concatenate(
            [jnp.concatenate([picked[0][4], none], axis=1), jnp.concatenate([none, picked[1][4]], axis=1)], axis=0
        )
        stored = jnp.concatenate([turned_ref[r + i, 4 * BLOCK :] for i in range(2)], axis=0)
        rest = jnp.dot(fifth, stored, preferred_element_type=jnp.float32)
        return most[0] + rest[:rows], most[1] + rest[rows:]

    for r in range(0, NBLOCK, 2):
        for b, source in zip((r, r + 1), sources(r, rounded_ref)):
            adv = adv_ref[b]
            field = adv + RELAX * (source - damping_ref[b : b + 1, :] * adv * jnp.abs(adv))
            speed = speeds_ref[b : b + 1, :]
            up = jnp.broadcast_to(upward_ref[b : b + 1, :], (8, 128)) == 1
            moved = []
            for k in range(2):
                here = field[8 * k + 8 : 8 * k + 16]
                chosen = jnp.where(up, field[8 * k : 8 * k + 8], field[8 * k + 16 : 8 * k + 24])
                moved.append(here - courant[k + 1] * speed * (here - chosen))
            moved = jnp.concatenate(moved, axis=0)
            adv2_ref[b] = moved
            rounded2_ref[b] = moved.astype(jnp.bfloat16)

    for r in range(0, NBLOCK, 2):
        for b, source in zip((r, r + 1), sources(r, rounded2_ref)):
            d, h = divmod(b, 2)
            adv = adv2_ref[b]
            last = adv + RELAX * (source - damping_ref[b : b + 1, :] * adv * jnp.abs(adv))
            for k in range(2):
                tile = 3 * (2 * d + k)
                rows = last[8 * k : 8 * k + 6]
                if h == 0:
                    out_ref[tile] = rows[0:4]
                    out_ref[tile + 1, 0:2, :] = rows[4:6]
                else:
                    out_ref[tile + 1, 2:4, :] = rows[0:2]
                    out_ref[tile + 2] = rows[2:6]


def unpack_kernel(msg_ref, out_hbm, out_ref, sems):
    each = PEERS // PIECES
    copies = []
    for i in range(PIECES):
        for j in range(each * i, each * i + each):
            row = COLS * j
            out_ref[row : row + 4, 0:128] = msg_ref[3 * j]
            out_ref[row + 4 : row + 6, 0:128] = msg_ref[3 * j + 1, 0:2, :]
            out_ref[row : row + 2, 128:256] = msg_ref[3 * j + 1, 2:4, :]
            out_ref[row + 2 : row + 6, 128:256] = msg_ref[3 * j + 2]
        part = pl.ds(COLS * each * i, COLS * each)
        copies.append(pltpu.make_async_copy(out_ref.at[part], out_hbm.at[part], sems.at[i]))
        copies[i].start()
    for copy in copies:
        copy.wait()


def vmem():
    return pl.BlockSpec(memory_space=pltpu.VMEM)


def hbm():
    return pl.BlockSpec(memory_space=pltpu.HBM)


def in_hbm(array):
    return pltpu.with_memory_space_constraint(array, pltpu.HBM)


PARAMS = dict(compiler_params=pltpu.CompilerParams(vmem_limit_bytes=VMEM_LIMIT))


def on_device(phonons, speeds, upward, courant, blocks, block_cols, damping):
    zs = lax.axis_size("z")
    even = [pair for i in range(0, zs - 1, 2) for pair in ((i, i + 1), (i + 1, i))]
    odd = [pair for i in range(1, zs - 1, 2) for pair in ((i, i + 1), (i + 1, i))]
    cells = jnp.transpose(phonons.reshape(256, 192))
    msg_type = jax.ShapeDtypeStruct((UNITS * PEERS, 2, 128), jnp.float32)

    msg = pl.pallas_call(
        pack_kernel,
        out_shape=msg_type,
        in_specs=[hbm()] * 2,
        out_specs=vmem(),
        scratch_shapes=[pltpu.VMEM((192, 256), jnp.float32), pltpu.VMEM((1, 192), jnp.float32), pltpu.SemaphoreType.DMA((PIECES + 1,))],
        **PARAMS,
    )(in_hbm(cells), in_hbm(courant))
    rec = lax.all_to_all(msg, PLANE, split_axis=0, concat_axis=0, tiled=True)
    halo = pl.pallas_call(
        halo_kernel, out_shape=jax.ShapeDtypeStruct((HALO_ROWS, 128), jnp.float32), in_specs=[vmem()], out_specs=vmem(), **PARAMS
    )(rec)
    even_got = lax.ppermute(halo, "z", even)
    odd_got = lax.ppermute(halo, "z", odd)
    vector = jax.ShapeDtypeStruct((NBLOCK, 128), jnp.float32)
    prepared = pl.pallas_call(
        prepare_kernel,
        out_shape=[
            jax.ShapeDtypeStruct((NBLOCK, NNZ * BLOCK, BLOCK), jnp.bfloat16),
            vector,
            jax.ShapeDtypeStruct((NBLOCK, 128), jnp.int32),
            vector,
        ],
        in_specs=[pl.BlockSpec(memory_space=pl.ANY)] + [hbm()] * 4,
        out_specs=[vmem()] * 4,
        scratch_shapes=[pltpu.VMEM((NBLOCK, NNZ, BLOCK, BLOCK), jnp.bfloat16), pltpu.SemaphoreType.DMA((PARTS + 3,))],
        cost_estimate=pl.CostEstimate(flops=0, bytes_accessed=11_000_000, transcendentals=0),
        **PARAMS,
    )(halo, *(in_hbm(a) for a in (blocks, speeds.reshape(NBLOCK, 128), upward.reshape(NBLOCK, 128), damping.reshape(NBLOCK, 128))))
    back = pl.pallas_call(
        steps_kernel,
        out_shape=jax.ShapeDtypeStruct((3 * PEERS, 4, 128), jnp.float32),
        in_specs=[vmem()] * 8,
        out_specs=vmem(),
        scratch_shapes=[
            pltpu.VMEM((NBLOCK, 32, 128), jnp.float32),
            pltpu.VMEM((NBLOCK, 32, 128), jnp.bfloat16),
            pltpu.VMEM((NBLOCK, 16, 128), jnp.float32),
            pltpu.VMEM((NBLOCK, 16, 128), jnp.bfloat16),
        ],
        **PARAMS,
    )(jnp.transpose(block_cols), halo, even_got, odd_got, *prepared)
    got = lax.all_to_all(back, PLANE, split_axis=0, concat_axis=0, tiled=True)
    out = pl.pallas_call(
        unpack_kernel,
        out_shape=jax.ShapeDtypeStruct((192, 256), jnp.float32),
        in_specs=[vmem()],
        out_specs=hbm(),
        scratch_shapes=[pltpu.VMEM((192, 256), jnp.float32), pltpu.SemaphoreType.DMA((PIECES,))],
        **PARAMS,
    )(got)
    return jnp.transpose(out).reshape(256, 1, 192)


def solution(mesh):
    fine = Mesh(mesh.devices.reshape(2, 4, 2, 32, 2), ("xh", "y", "core", "z", "xl"))
    return jax.shard_map(
        on_device,
        mesh=fine,
        in_specs=(P(MODE, ("z", "xl"), None), P(), P(), P(("z", "xl"), None), P(), P(), P()),
        out_specs=P(MODE, ("z", "xl"), None),
        check_vma=False,
    )
```

```python
import jax
import jax.numpy as jnp
from jax import lax
from jax.experimental import pallas as pl
from jax.experimental.pallas import tpu as pltpu
from jax.sharding import Mesh, PartitionSpec as P

MODE = ("xh", "y", "core")
PLANE = ("xh", "xl", "y", "core")
PEERS = 32
UNITS = 7
PIECES = 4
COLS = 6
NBLOCK = 32
NNZ = 5
BLOCK = 128
HALO_ROWS = 392
CHUNK = 4
PARTS = NBLOCK // CHUNK
RELAX = 0.25
VMEM_LIMIT = 32 * 1024 * 1024


def peer(mode, xl):
    return mode // 8 * 16 + 8 * xl + mode % 8


def pack_kernel(x_hbm, c_hbm, msg_ref, x_ref, c_ref, sems):
    each = PEERS // PIECES
    courant = pltpu.make_async_copy(c_hbm, c_ref, sems.at[PIECES])
    copies = []
    for i in range(PIECES):
        part = pl.ds(COLS * each * i, COLS * each)
        copies.append(pltpu.make_async_copy(x_hbm.at[part], x_ref.at[part], sems.at[i]))
    for copy in copies + [courant]:
        copy.start()
    for i in range(PIECES):
        copies[i].wait()
        for j in range(each * i, each * i + each):
            for h in range(2):
                for p in range(3):
                    row = COLS * j + 2 * p
                    msg_ref[UNITS * j + 3 * h + p] = x_ref[row : row + 2, 128 * h : 128 * h + 128]
    courant.wait()
    for j in range(PEERS):
        msg_ref[UNITS * j + 6, 0:1, 0:6] = c_ref[0:1, COLS * j : COLS * j + 6]


def halo_kernel(rec_ref, out_ref):
    for d in range(16):
        for xl in range(2):
            for h in range(2):
                for p in range(3):
                    row = 24 * d + 12 * xl + 6 * h + 2 * p
                    out_ref[row : row + 2, :] = rec_ref[UNITS * peer(d, xl) + 3 * h + p]
    for xl in range(2):
        out_ref[384 + xl : 385 + xl, :] = rec_ref[UNITS * peer(0, xl) + 6, 0:1, :]


def on_rows(row):
    lane = lax.broadcasted_iota(jnp.int32, (8, 128), 1)
    cell = lax.broadcasted_iota(jnp.int32, (8, 128), 0)
    picked = jnp.where(lane == cell, jnp.broadcast_to(row, (8, 128)), 0.0)
    return jnp.broadcast_to(jnp.sum(picked, axis=1, keepdims=True), (8, 128))


def prepare_kernel(
    _, blocks_hbm, speeds_hbm, upward_hbm, damping_hbm,
    turned_ref, speeds_ref, upward_ref, damping_ref, blocks_ref, sems,
):
    vectors = [
        pltpu.make_async_copy(speeds_hbm, speeds_ref, sems.at[PARTS]),
        pltpu.make_async_copy(upward_hbm, upward_ref, sems.at[PARTS + 1]),
        pltpu.make_async_copy(damping_hbm, damping_ref, sems.at[PARTS + 2]),
    ]
    copies = []
    for i in range(PARTS):
        part = pl.ds(CHUNK * i, CHUNK)
        copies.append(pltpu.make_async_copy(blocks_hbm.at[part], blocks_ref.at[part], sems.at[i]))
    for copy in copies + vectors:
        copy.start()
    for i in range(PARTS):
        copies[i].wait()
        for r in range(CHUNK * i, CHUNK * i + CHUNK):
            for k in range(NNZ):
                turned_ref[r, BLOCK * k : BLOCK * k + BLOCK, :] = blocks_ref[r, k].T
    for copy in vectors:
        copy.wait()


def steps_kernel(
    cols_ref, own_ref, even_ref, odd_ref, turned_ref, speeds_ref, upward_ref, damping_ref,
    out_ref, adv_ref, rounded_ref, adv2_ref, rounded2_ref,
):
    is_odd = lax.axis_index("z") % 2 == 1

    def low(row, rows):
        return jnp.where(is_odd, even_ref[row : row + rows, :], odd_ref[row : row + rows, :])

    def high(row, rows):
        return jnp.where(is_odd, odd_ref[row : row + rows, :], even_ref[row : row + rows, :])

    courant = [
        on_rows(low(385, 1)),
        on_rows(own_ref[384:385, :]),
        on_rows(own_ref[385:386, :]),
        on_rows(high(384, 1)),
    ]

    for b in range(NBLOCK):
        d, h = divmod(b, 2)
        row = 24 * d + 6 * h
        layers = [
            low(row, 8),
            low(row + 12, 8),
            own_ref[row : row + 8, :],
            own_ref[row + 12 : row + 20, :],
            high(row, 8),
            high(row + 12, 8),
        ]
        speed = speeds_ref[b : b + 1, :]
        up = jnp.broadcast_to(upward_ref[b : b + 1, :], (8, 128)) == 1
        moved = []
        for k in range(4):
            here = layers[k + 1]
            chosen = jnp.where(up, layers[k], layers[k + 2])
            moved.append(here - courant[k] * speed * (here - chosen))
        moved = jnp.concatenate(moved, axis=0)
        adv_ref[b] = moved
        rounded_ref[b] = moved.astype(jnp.bfloat16)

    def sources(r, values_ref):
        rows = values_ref.shape[1]
        picked = [[values_ref[cols_ref[k, r + i]] for k in range(NNZ)] for i in range(2)]
        most = [
            jnp.dot(jnp.concatenate(picked[i][:4], axis=1), turned_ref[r + i, : 4 * BLOCK], preferred_element_type=jnp.float32)
            for i in range(2)
        ]
        none = jnp.zeros((rows, BLOCK), jnp.bfloat16)
        fifth = jnp.concatenate(
            [jnp.concatenate([picked[0][4], none], axis=1), jnp.concatenate([none, picked[1][4]], axis=1)], axis=0
        )
        stored = jnp.concatenate([turned_ref[r + i, 4 * BLOCK :] for i in range(2)], axis=0)
        rest = jnp.dot(fifth, stored, preferred_element_type=jnp.float32)
        return most[0] + rest[:rows], most[1] + rest[rows:]

    for r in range(0, NBLOCK, 2):
        for b, source in zip((r, r + 1), sources(r, rounded_ref)):
            adv = adv_ref[b]
            field = adv + RELAX * (source - damping_ref[b : b + 1, :] * adv * jnp.abs(adv))
            speed = speeds_ref[b : b + 1, :]
            up = jnp.broadcast_to(upward_ref[b : b + 1, :], (8, 128)) == 1
            moved = []
            for k in range(2):
                here = field[8 * k + 8 : 8 * k + 16]
                chosen = jnp.where(up, field[8 * k : 8 * k + 8], field[8 * k + 16 : 8 * k + 24])
                moved.append(here - courant[k + 1] * speed * (here - chosen))
            moved = jnp.concatenate(moved, axis=0)
            adv2_ref[b] = moved
            rounded2_ref[b] = moved.astype(jnp.bfloat16)

    for r in range(0, NBLOCK, 2):
        for b, source in zip((r, r + 1), sources(r, rounded2_ref)):
            d, h = divmod(b, 2)
            adv = adv2_ref[b]
            last = adv + RELAX * (source - damping_ref[b : b + 1, :] * adv * jnp.abs(adv))
            for k in range(2):
                tile = 3 * peer(d, k)
                rows = last[8 * k : 8 * k + 6]
                if h == 0:
                    out_ref[tile] = rows[0:4]
                    out_ref[tile + 1, 0:2, :] = rows[4:6]
                else:
                    out_ref[tile + 1, 2:4, :] = rows[0:2]
                    out_ref[tile + 2] = rows[2:6]


def unpack_kernel(msg_ref, out_hbm, out_ref, sems):
    each = PEERS // PIECES
    copies = []
    for i in range(PIECES):
        for j in range(each * i, each * i + each):
            row = COLS * j
            out_ref[row : row + 4, 0:128] = msg_ref[3 * j]
            out_ref[row + 4 : row + 6, 0:128] = msg_ref[3 * j + 1, 0:2, :]
            out_ref[row : row + 2, 128:256] = msg_ref[3 * j + 1, 2:4, :]
            out_ref[row + 2 : row + 6, 128:256] = msg_ref[3 * j + 2]
        part = pl.ds(COLS * each * i, COLS * each)
        copies.append(pltpu.make_async_copy(out_ref.at[part], out_hbm.at[part], sems.at[i]))
        copies[i].start()
    for copy in copies:
        copy.wait()


def vmem():
    return pl.BlockSpec(memory_space=pltpu.VMEM)


def hbm():
    return pl.BlockSpec(memory_space=pltpu.HBM)


def in_hbm(array):
    return pltpu.with_memory_space_constraint(array, pltpu.HBM)


PARAMS = dict(compiler_params=pltpu.CompilerParams(vmem_limit_bytes=VMEM_LIMIT))


def on_device(phonons, speeds, upward, courant, blocks, block_cols, damping):
    zs = lax.axis_size("z")
    even = [pair for i in range(0, zs - 1, 2) for pair in ((i, i + 1), (i + 1, i))]
    odd = [pair for i in range(1, zs - 1, 2) for pair in ((i, i + 1), (i + 1, i))]
    cells = jnp.transpose(phonons.reshape(256, 192))
    msg_type = jax.ShapeDtypeStruct((UNITS * PEERS, 2, 128), jnp.float32)

    msg = pl.pallas_call(
        pack_kernel,
        out_shape=msg_type,
        in_specs=[hbm()] * 2,
        out_specs=vmem(),
        scratch_shapes=[pltpu.VMEM((192, 256), jnp.float32), pltpu.VMEM((1, 192), jnp.float32), pltpu.SemaphoreType.DMA((PIECES + 1,))],
        **PARAMS,
    )(in_hbm(cells), in_hbm(courant))
    rec = lax.all_to_all(msg, PLANE, split_axis=0, concat_axis=0, tiled=True)
    halo = pl.pallas_call(
        halo_kernel, out_shape=jax.ShapeDtypeStruct((HALO_ROWS, 128), jnp.float32), in_specs=[vmem()], out_specs=vmem(), **PARAMS
    )(rec)
    even_got = lax.ppermute(halo, "z", even)
    odd_got = lax.ppermute(halo, "z", odd)
    vector = jax.ShapeDtypeStruct((NBLOCK, 128), jnp.float32)
    prepared = pl.pallas_call(
        prepare_kernel,
        out_shape=[
            jax.ShapeDtypeStruct((NBLOCK, NNZ * BLOCK, BLOCK), jnp.bfloat16),
            vector,
            jax.ShapeDtypeStruct((NBLOCK, 128), jnp.int32),
            vector,
        ],
        in_specs=[pl.BlockSpec(memory_space=pl.ANY)] + [hbm()] * 4,
        out_specs=[vmem()] * 4,
        scratch_shapes=[pltpu.VMEM((NBLOCK, NNZ, BLOCK, BLOCK), jnp.bfloat16), pltpu.SemaphoreType.DMA((PARTS + 3,))],
        cost_estimate=pl.CostEstimate(flops=0, bytes_accessed=11_000_000, transcendentals=0),
        **PARAMS,
    )(halo, *(in_hbm(a) for a in (blocks, speeds.reshape(NBLOCK, 128), upward.reshape(NBLOCK, 128), damping.reshape(NBLOCK, 128))))
    back = pl.pallas_call(
        steps_kernel,
        out_shape=jax.ShapeDtypeStruct((3 * PEERS, 4, 128), jnp.float32),
        in_specs=[vmem()] * 8,
        out_specs=vmem(),
        scratch_shapes=[
            pltpu.VMEM((NBLOCK, 32, 128), jnp.float32),
            pltpu.VMEM((NBLOCK, 32, 128), jnp.bfloat16),
            pltpu.VMEM((NBLOCK, 16, 128), jnp.float32),
            pltpu.VMEM((NBLOCK, 16, 128), jnp.bfloat16),
        ],
        **PARAMS,
    )(jnp.transpose(block_cols), halo, even_got, odd_got, *prepared)
    got = lax.all_to_all(back, PLANE, split_axis=0, concat_axis=0, tiled=True)
    out = pl.pallas_call(
        unpack_kernel,
        out_shape=jax.ShapeDtypeStruct((192, 256), jnp.float32),
        in_specs=[vmem()],
        out_specs=hbm(),
        scratch_shapes=[pltpu.VMEM((192, 256), jnp.float32), pltpu.SemaphoreType.DMA((PIECES,))],
        **PARAMS,
    )(got)
    return jnp.transpose(out).reshape(256, 1, 192)


def solution(mesh):
    fine = Mesh(mesh.devices.reshape(2, 4, 2, 32, 2), ("xh", "y", "core", "z", "xl"))
    return jax.shard_map(
        on_device,
        mesh=fine,
        in_specs=(P(MODE, ("z", "xl"), None), P(), P(), P(("z", "xl"), None), P(), P(), P()),
        out_specs=P(MODE, ("z", "xl"), None),
        check_vma=False,
    )
```
